256 devices in a mesh: seq: 64 (over y_lo, x, z), head: 4 (over y_hi, core).
Axes of the slice: x: 4, y: 4 (y_hi: 2, y_lo: 2; y = y_hi * 2 + y_lo), z: 8, core: 2. Of those that a mesh axis runs over, the one named last changes fastest.
Arguments:
- query_rows: bfloat16 [32768, 2560], P('seq', 'head'), may hold values from -8 to 8
- key_rows: bfloat16 [32768, 2560], P('seq', 'head'), may hold values from -8 to 8
- value_rows: bfloat16 [32768, 2560], P('seq', 'head'), may hold values from -3 to 3
- out_weight: bfloat16 [2560, 2560], P('head'), may hold values from -0.125 to 0.125
- cotangent: bfloat16 [32768, 2560], P('seq', 'head'), may hold values from -6 to 6
- offsets: int32 [2, 32], P(None, 'head'), may hold values from 0 to 63, as said below
Outputs:
- attended: bfloat16 [32768, 2560], P('seq', 'head')
- grad_query: bfloat16 [32768, 2560], P('seq', 'head')
- grad_key: bfloat16 [32768, 2560], P('seq', 'head')
- grad_value: bfloat16 [32768, 2560], P('seq', 'head')
The draws below stay inside these ranges and needn't reach their ends.
Inputs may be any that keep to these rules, and one draw needn't show every extreme that they name: `offsets`: row 0 holds each head's offset at the middle level, below 4; row 1 the offset at the sequence-wide level, below 64.
All inputs are finite; a program needn't handle non-finite values.
Results may differ from the reference program's by a relative error of at most 0.025.
Values may be sent and summed in bfloat16 or wider, within the bound.
No kernel may reach another device: no remote copies, remote signals or barrier semaphores. Data moves between devices by JAX's collectives and lax.ppermute only.
A program may use at most 128 MiB of HBM per device.

```python
import math
import jax
import jax.numpy as jnp
from jax import lax

HEADS = 32
HEAD_DIM = 80
TOK_DEV = 512
NEAR_RATE = 4
WIDTH = 2560
TOKENS = 32768
FAR_RATE = 64


def draw_query_rows(key, part):
    key = jax.random.fold_in(key, 1)
    drawn = jax.random.normal(key, (TOKENS, HEADS * HEAD_DIM), jnp.float32)
    return jnp.clip(drawn, -8.0, 8.0).astype(jnp.bfloat16)


def draw_key_rows(key, part):
    key = jax.random.fold_in(key, 2)
    drawn = jax.random.normal(key, (TOKENS, HEADS * HEAD_DIM), jnp.float32)
    return jnp.clip(drawn, -6.0, 6.0).astype(jnp.bfloat16)


def draw_offsets(key, part):
    key = jax.random.fold_in(key, 7)
    first_key, second_key, third_key, fourth_key = jax.random.split(key, 4)
    near_offsets = jax.random.randint(first_key, (HEADS,), 0, NEAR_RATE)
    far_offsets = jax.random.randint(second_key, (HEADS,), 0, FAR_RATE)
    far_offsets = far_offsets.at[jax.random.randint(third_key, (), 0, HEADS)].set(FAR_RATE - 1)
    near_offsets = near_offsets.at[jax.random.randint(fourth_key, (), 0, HEADS)].set(0)
    return jnp.stack([near_offsets, far_offsets]).astype(jnp.int32)


def block_scale(rng, dims, cuts, smallest, high):
    loudness, own = 1.0, jax.random.fold_in(rng, 6)
    for dim, parts in cuts:
        heights = jnp.exp(jax.random.uniform(jax.random.fold_in(own, dim), (parts,), jnp.float32, smallest / len(cuts), high / len(cuts)))
        loudness = loudness * jnp.repeat(heights, dims[dim] // parts).reshape([-1 if axis == dim else 1 for axis in range(len(dims))])
    return loudness


def noise(own_key, dims, width, reach, cuts=(), kind=jnp.bfloat16):
    drawn = jax.random.normal(own_key, dims, jnp.float32) * width
    if len(cuts) > 0:
        drawn = block_scale(own_key, dims, cuts, -0.22, 0.18) * drawn
    return jnp.clip(drawn, min=-reach, max=reach).astype(kind)


def setup_inputs(seed: int = 0) -> dict:
    seeds = jax.random.split(jax.random.key(seed), 7)
    return {
        "query_rows": draw_query_rows(jax.random.fold_in(seeds[6], 71), 0),
        "key_rows": draw_key_rows(jax.random.fold_in(seeds[6], 71), 0),
        "value_rows": noise(seeds[2], (TOKENS, HEADS * HEAD_DIM), 0.5, 3.0, ((0, 64), (1, 4))),
        "out_weight": noise(seeds[3], (HEADS * HEAD_DIM, WIDTH), (HEADS * HEAD_DIM) ** -0.5, 0.125, ((0, 4),)),
        "cotangent": noise(seeds[4], (TOKENS, WIDTH), 1.0, 6.0, ((0, 64), (1, 4))),
        "offsets": draw_offsets(jax.random.fold_in(seeds[6], 71), 0),
    }


def select(matrix, dilation, offset):
    grid_view = matrix.reshape((matrix.shape[0] // dilation, dilation) + matrix.shape[1:])
    return lax.dynamic_index_in_dim(grid_view, offset, axis=1, keepdims=False)

def spread(matrix, dilation, offset, filler):
    pick_mask = (jnp.arange(dilation) == offset).reshape((1, dilation) + (1,) * (matrix.ndim - 1))
    widened = jnp.where(pick_mask, matrix[:, None], filler)
    return widened.reshape((matrix.shape[0] * dilation,) + matrix.shape[1:])

def one_head(inputs):
    head_queries, head_keys, head_values, head_grads, near_offset, far_offset = inputs
    score_scale = 1.0 / math.sqrt(HEAD_DIM)
    causal = jnp.arange(TOK_DEV)[:, None] >= jnp.arange(TOK_DEV)[None, :]
    levels = ((1, jnp.zeros((), jnp.int32)), (NEAR_RATE, near_offset), (FAR_RATE, far_offset))
    gathered = []
    log_total = None
    for dilation, offset in levels:
        level_queries = select(head_queries, dilation, offset).reshape(-1, TOK_DEV, HEAD_DIM).astype(jnp.float32)
        level_keys = select(head_keys, dilation, offset).reshape(-1, TOK_DEV, HEAD_DIM).astype(jnp.float32)
        level_values = select(head_values, dilation, offset).reshape(-1, TOK_DEV, HEAD_DIM).astype(jnp.float32)
        scores = jnp.einsum('sad,sbd->sab', level_queries, level_keys) * score_scale
        scores = jnp.where(causal[None], scores, -jnp.inf)
        row_max = lax.optimization_barrier(jnp.max(scores, axis=2, keepdims=True))
        log_norm = row_max[..., 0] + jnp.log(lax.optimization_barrier(jnp.sum(jnp.exp(scores - row_max), axis=2)))
        placed = spread(log_norm.reshape(-1), dilation, offset, -jnp.inf)
        log_total = placed if log_total is None else jnp.logaddexp(log_total, placed)
        gathered.append((dilation, offset, level_queries, level_keys, level_values, scores))
    attended = jnp.zeros((TOKENS, HEAD_DIM), jnp.float32)
    stored = []
    for dilation, offset, level_queries, level_keys, level_values, scores in gathered:
        row_total = select(log_total, dilation, offset).reshape(-1, TOK_DEV)
        weights = jnp.exp(scores - row_total[..., None])
        rounded = lax.optimization_barrier(weights.astype(jnp.bfloat16)).astype(jnp.float32)
        level_out = jnp.einsum('sab,sbd->sad', rounded, level_values)
        attended = attended + spread(level_out.reshape(-1, HEAD_DIM), dilation, offset, 0.0)
        stored.append((dilation, offset, level_queries, level_keys, level_values, weights, rounded))
    attended = attended.astype(jnp.bfloat16)
    grads_float = head_grads.astype(jnp.float32)
    deltas = lax.optimization_barrier(jnp.sum(grads_float * attended.astype(jnp.float32), axis=1))
    query_grad = jnp.zeros((TOKENS, HEAD_DIM), jnp.float32)
    key_grad = jnp.zeros((TOKENS, HEAD_DIM), jnp.float32)
    value_grad = jnp.zeros((TOKENS, HEAD_DIM), jnp.float32)
    for dilation, offset, level_queries, level_keys, level_values, weights, rounded in stored:
        level_grads_out = select(grads_float, dilation, offset).reshape(-1, TOK_DEV, HEAD_DIM)
        level_deltas = select(deltas, dilation, offset).reshape(-1, TOK_DEV)
        grad_weights = jnp.einsum('sad,sbd->sab', level_grads_out, level_values)
        grad_scores = (weights * (grad_weights - level_deltas[..., None]) * score_scale).astype(jnp.bfloat16)
        grad_scores = lax.optimization_barrier(grad_scores).astype(jnp.float32)
        query_part = jnp.einsum('sab,sbd->sad', grad_scores, level_keys)
        key_part = jnp.einsum('sab,sad->sbd', grad_scores, level_queries)
        value_part = jnp.einsum('sab,sad->sbd', rounded, level_grads_out)
        query_grad = query_grad + spread(query_part.reshape(-1, HEAD_DIM), dilation, offset, 0.0)
        key_grad = key_grad + spread(key_part.reshape(-1, HEAD_DIM), dilation, offset, 0.0)
        value_grad = value_grad + spread(value_part.reshape(-1, HEAD_DIM), dilation, offset, 0.0)
    return (attended, query_grad.astype(jnp.bfloat16), key_grad.astype(jnp.bfloat16), value_grad.astype(jnp.bfloat16))

def heads_first(matrix):
    return matrix.reshape(TOKENS, HEADS, HEAD_DIM).transpose(1, 0, 2)

def heads_last(matrix):
    return matrix.transpose(1, 0, 2).reshape(TOKENS, HEADS * HEAD_DIM)

def reference(query_rows, key_rows, value_rows, out_weight, cotangent, offsets):
    grad_attended = jnp.dot(cotangent, out_weight.T, preferred_element_type=jnp.float32).astype(jnp.bfloat16)
    results = lax.map(one_head, (heads_first(query_rows), heads_first(key_rows), heads_first(value_rows), heads_first(grad_attended), offsets[0].astype(jnp.int32), offsets[1].astype(jnp.int32)))
    return (heads_last(results[0]), heads_last(results[1]), heads_last(results[2]), heads_last(results[3]))
```

```python
import functools
import math

import jax
import jax.numpy as jnp
from jax import lax
from jax.experimental import pallas as pl
from jax.experimental.pallas import tpu as pltpu
from jax.sharding import PartitionSpec as P

NEAR = 4
F32 = jnp.float32
BF16 = jnp.bfloat16
LOG2E = math.log2(math.e)
NEG = float("-inf")


def nn(a, b):
    return lax.dot_general(a, b, (((1,), (0,)), ((), ())), preferred_element_type=F32)


def nt(a, b):
    return lax.dot_general(a, b, (((1,), (1,)), ((), ())), preferred_element_type=F32)


def tn(a, b):
    return lax.dot_general(a, b, (((0,), (0,)), ((), ())), preferred_element_type=F32)


def iota(shape, dim):
    return lax.broadcasted_iota(jnp.int32, shape, dim)


def one_hot(mask):
    return jnp.where(mask, 1.0, 0.0).astype(BF16)


def pick_matrix(tokens, count, offset):
    rate = tokens // count
    return one_hot(iota((tokens, count), 0) == iota((tokens, count), 1) * rate + offset)


def place_matrix(tokens, count, offset, rows=None):
    rate = tokens // count
    rows = rows or count
    return one_hot(iota((rows, tokens), 1) == iota((rows, tokens), 0) * rate + offset)


def split3(x):
    high = x.astype(BF16).astype(F32)
    rest = x - high
    middle = rest.astype(BF16).astype(F32)
    return high, middle, rest - middle


def log2_add(a, b):
    top = jnp.maximum(a, b)
    return top + jnp.log(jnp.exp2(a - top) + jnp.exp2(b - top)) * LOG2E


def causal_mask(size):
    return iota((size, size), 0) <= iota((size, size), 1)


def halves(tokens):
    half = tokens // 2
    return half, ((0, slice(0, half)), (1, slice(half, tokens)))


def forward(qt, kt, vt, factor, diag):
    tokens = qt.shape[1]
    half, blocks = halves(tokens)
    outs, norms = [], []
    for index, cols in blocks:
        keys = (index + 1) * half
        scores = tn(kt[:, :keys], qt[:, cols])
        last = jnp.where(diag, scores[keys - half :], NEG)
        parts = [last] if index == 0 else [scores[:half], last]
        top = functools.reduce(
            jnp.maximum, [jnp.max(part, axis=0, keepdims=True) for part in parts]
        )
        top = top * factor
        probs = [jnp.exp2(part * factor - top) for part in parts]
        total = sum(jnp.sum(part, axis=0, keepdims=True) for part in probs)
        packed = [part.astype(BF16) for part in probs]
        packed = packed[0] if index == 0 else jnp.concatenate(packed, axis=0)
        outs.append(nn(vt[:, :keys], packed) / total)
        norms.append(top + jnp.log(total) * LOG2E)
    return jnp.concatenate(outs, axis=1), jnp.concatenate(norms, axis=1)


def backward(qt, kt, vt, gt, norm, delta, factor, scale, diag):
    tokens = qt.shape[1]
    half, blocks = halves(tokens)
    dq = []
    for index, cols in blocks:
        keys = (index + 1) * half
        scores = tn(kt[:, :keys], qt[:, cols]) * factor - norm[:, cols]
        last = jnp.where(diag, jnp.exp2(scores[keys - half :]), 0.0)
        if index == 0:
            probs = last
        else:
            probs = jnp.concatenate([jnp.exp2(scores[:half]), last], axis=0)
        dprobs = tn(vt[:, :keys], gt[:, cols])
        dscores = (probs * (dprobs - delta[:, cols])).astype(BF16)
        dq.append(nn(kt[:, :keys], dscores) * scale)
        dk_part = nt(qt[:, cols], dscores) * scale
        dv_part = nt(gt[:, cols], probs.astype(BF16))
        if index == 0:
            dk, dv = dk_part, dv_part
        else:
            dk = jnp.concatenate([dk + dk_part[:, :half], dk_part[:, half:]], axis=1)
            dv = jnp.concatenate([dv + dv_part[:, :half], dv_part[:, half:]], axis=1)
    return jnp.concatenate(dq, axis=1), dk, dv


def prep_kernel(heads, sc, q, k, v, qkvt, near_q, near_kv, far_msg):
    tokens, width = q.shape
    d = width // heads
    for slot, ref in enumerate((q, k, v)):
        turned = ref[...].T
        for h in range(heads):
            qkvt[h, slot * d : (slot + 1) * d, :] = turned[h * d : (h + 1) * d]
    fill = qkvt.shape[1] - 3 * d
    near_count = tokens // NEAR
    for h in range(heads):
        qkvt[h, 3 * d :, :] = jnp.zeros((fill, tokens), BF16)
        block = qkvt[h]
        near = nn(block[: 3 * d], pick_matrix(tokens, near_count, sc[h])).astype(BF16)
        near_q[h] = near[:d]
        near_kv[h] = near[d:]
        rows = nt(place_matrix(tokens, 8, sc[heads + h], 16), block)
        message = jnp.concatenate([rows[:8, :128], rows[:8, 128:]], axis=0).astype(BF16)
        for copy in range(far_msg.shape[0]):
            far_msg[copy, h] = message


def local_kernel(heads, d, factor, qkvt, out, norm):
    tokens = qkvt.shape[2]
    diag = causal_mask(tokens // 2)
    for h in range(heads):
        o, n = forward(
            qkvt[h, :d], qkvt[h, d : 2 * d], qkvt[h, 2 * d : 3 * d], factor, diag
        )
        out[h] = o
        norm[h : h + 1, :] = n


def far_forward_kernel(d, factor, sc, got, qkvt, out, norm, msg, turned):
    rows = got[...].astype(F32)
    tokens = rows.shape[0] * 8
    wide = jnp.concatenate(
        [rows[:, :8].reshape(tokens, 128), rows[:, 8:].reshape(tokens, 128)], axis=1
    )
    block = wide.T.astype(BF16)
    qkvt[...] = block
    diag = causal_mask(tokens // 2)
    o, n = forward(block[:d], block[d : 2 * d], block[2 * d : 3 * d], factor, diag)
    out[...] = o
    norm[...] = jnp.broadcast_to(n, norm.shape)
    stack = jnp.concatenate(
        [o, jnp.broadcast_to(n, (8, tokens)), jnp.zeros((120 - d, tokens), F32)], axis=0
    )
    turned[...] = stack.T
    msg[...] = turned[pl.ds(pl.multiple_of(sc[17] * 64, 64), 64), :]


def near_bias(sc, slot):
    return jnp.where(sc[16] >= slot, 0.0, NEG).astype(F32)


def near_scores(sc, kt, qt, diag):
    count = qt.shape[1]
    scores = tn(kt, qt)
    parts = [jnp.where(diag, scores[:count], NEG)]
    for slot in range(1, NEAR):
        parts.append(scores[slot * count : (slot + 1) * count] + near_bias(sc, slot))
    return parts


def near_forward_kernel(heads, d, factor, sc, q, kv0, kv1, kv2, kv3, out, norm):
    count = q.shape[2]
    diag = causal_mask(count)
    for h in range(heads):
        kv = jnp.concatenate([kv0[h], kv1[h], kv2[h], kv3[h]], axis=1)
        parts = near_scores(sc, kv[:d], q[h], diag)
        top = functools.reduce(
            jnp.maximum, [jnp.max(part, axis=0, keepdims=True) for part in parts]
        )
        top = top * factor
        probs = [jnp.exp2(part * factor - top) for part in parts]
        total = sum(jnp.sum(part, axis=0, keepdims=True) for part in probs)
        packed = jnp.concatenate([part.astype(BF16) for part in probs], axis=0)
        out[h] = (nn(kv[d:], packed) / total).astype(BF16)
        norm[h : h + 1, :] = top + jnp.log(total) * LOG2E


def mix_kernel(
    heads, d, sc, w, c0, c1, c2, c3, l_out, l_norm, n_out, n_norm, gt, out, norm, msg
):
    tokens = c0.shape[0]
    width = heads * d
    grads = jnp.zeros((width, tokens), F32)
    for flip, ref in enumerate((c0, c1, c2, c3)):
        first = pl.multiple_of(jnp.bitwise_xor(sc[18], flip) * width, 128)
        grads = grads + nt(w[:, pl.ds(first, width)], ref[...])
    grads = grads.astype(BF16)
    gt[...] = grads
    count = tokens // NEAR
    lane = iota((1, tokens), 1)
    for h in range(heads):
        place = place_matrix(tokens, count, sc[h])
        terms = jnp.concatenate(split3(n_norm[h : h + 1, :]), axis=0)
        spread = jnp.sum(nn(terms.astype(BF16), place), axis=0, keepdims=True)
        near = jnp.where(lane % NEAR == sc[h], spread, NEG)
        mine = l_norm[h : h + 1, :]
        both = log2_add(mine, near)
        mixed = jnp.exp2(mine - both) * l_out[h] + jnp.exp2(near - both) * nn(
            n_out[h], place
        )
        out[h] = mixed
        norm[h : h + 1, :] = both
        g = grads[h * d : (h + 1) * d]
        product = jnp.sum(g.astype(F32) * mixed, axis=0, keepdims=True)
        stack = jnp.concatenate(
            [
                g.astype(F32),
                *split3(both),
                *split3(product),
                jnp.zeros((122 - d, tokens), F32),
            ],
            axis=0,
        ).astype(BF16)
        rows = nt(place_matrix(tokens, 8, sc[heads + h], 16), stack)[:8]
        for copy in range(msg.shape[0]):
            msg[copy, h] = rows


def total_kernel(
    heads, d, factor, scale, sc, gt, out, norm, far, nq, kv0, kv1, kv2, kv3,
    attended, all_norm, all_delta, own, back1, back2, back3, turned,
):
    tokens = gt.shape[1]
    count = tokens // NEAR
    diag = causal_mask(count)
    for h in range(heads):
        place = iota((8, tokens), 1) == iota((8, tokens), 0) * 64 + sc[heads + h]
        rows = far[h]
        spread = jnp.sum(jnp.where(place, rows[:, d : d + 1], 0.0), axis=0, keepdims=True)
        hit = iota((1, tokens), 1) % 64 == sc[heads + h]
        far_norm = jnp.where(hit, spread, NEG)
        mine = norm[h : h + 1, :]
        both = log2_add(mine, far_norm)
        far_out = tn(rows[:, :d].astype(BF16), one_hot(place))
        mixed = jnp.exp2(mine - both) * out[h] + jnp.exp2(far_norm - both) * far_out
        mixed = mixed.astype(BF16)
        turned[h * d : (h + 1) * d, :] = mixed
        g = gt[h * d : (h + 1) * d, :]
        delta = jnp.sum(g.astype(F32) * mixed.astype(F32), axis=0, keepdims=True)
        all_norm[h : h + 1, :] = both
        all_delta[h : h + 1, :] = delta
        stack = jnp.concatenate(
            [g.astype(F32), *split3(both), *split3(delta), jnp.zeros((10, tokens), F32)], axis=0
        ).astype(BF16)
        picked = nn(stack, pick_matrix(tokens, count, sc[h]))
        near_g = picked[:d].astype(BF16)
        near_norm = picked[d : d + 1] + picked[d + 1 : d + 2] + picked[d + 2 : d + 3]
        near_delta = picked[d + 3 : d + 4] + picked[d + 4 : d + 5] + picked[d + 5 : d + 6]
        kv = jnp.concatenate([kv0[h], kv1[h], kv2[h], kv3[h]], axis=1)
        q = nq[h]
        parts = near_scores(sc, kv[:d], q, diag)
        probs = jnp.concatenate(
            [jnp.exp2(part * factor - near_norm) for part in parts], axis=0
        )
        dprobs = tn(kv[d:], near_g)
        dscores = (probs * (dprobs - near_delta)).astype(BF16)
        own[h, :d] = (nn(kv[:d], dscores) * scale).astype(BF16)
        dk = (nt(q, dscores) * scale).astype(BF16)
        dv = nt(near_g, probs.astype(BF16)).astype(BF16)
        own[h, d : 2 * d] = dk[:, :count]
        own[h, 2 * d :] = dv[:, :count]
        for slot, ref in ((1, back1), (2, back2), (3, back3)):
            ref[h, :d] = dk[:, slot * count : (slot + 1) * count]
            ref[h, d:] = dv[:, slot * count : (slot + 1) * count]
    attended[...] = turned[...].T


def far_backward_kernel(d, factor, scale, sc, qkvt, out, norm, got, msg, turned):
    tokens = qkvt.shape[1]
    rows = got[...].reshape(tokens, 128).T
    gt = rows[:d].astype(BF16)
    rest_norm = rows[d : d + 1] + rows[d + 1 : d + 2] + rows[d + 2 : d + 3]
    rest_delta = rows[d + 3 : d + 4] + rows[d + 4 : d + 5] + rows[d + 5 : d + 6]
    mine = norm[:1, :]
    both = log2_add(mine, rest_norm)
    mine_delta = jnp.sum(rows[:d] * out[...], axis=0, keepdims=True)
    delta = jnp.exp2(mine - both) * mine_delta + jnp.exp2(rest_norm - both) * rest_delta
    dq, dk, dv = backward(
        qkvt[:d], qkvt[d : 2 * d], qkvt[2 * d : 3 * d], gt, both, delta, factor, scale,
        causal_mask(tokens // 2),
    )
    stack = jnp.concatenate([dq, dk, dv, jnp.zeros((256 - 3 * d, tokens), F32)], axis=0)
    turned[...] = stack.T
    msg[...] = turned[pl.ds(pl.multiple_of(sc[17] * 64, 64), 64), :]


def local_backward_kernel(heads, d, factor, scale, qkvt, gt, norm, delta, grads):
    tokens = gt.shape[1]
    diag = causal_mask(tokens // 2)
    for h in range(heads):
        dq, dk, dv = backward(
            qkvt[h, :d],
            qkvt[h, d : 2 * d],
            qkvt[h, 2 * d : 3 * d],
            gt[h * d : (h + 1) * d, :],
            norm[h : h + 1, :],
            delta[h : h + 1, :],
            factor,
            scale,
            diag,
        )
        grads[h, :d] = dq
        grads[h, d : 2 * d] = dk
        grads[h, 2 * d :] = dv


def final_kernel(heads, d, sc, grads, own, back1, back2, back3, far, dq, dk, dv, turned):
    tokens = grads.shape[2]
    count = tokens // NEAR
    for h in range(heads):
        near = own[h].astype(F32)
        came = back1[h].astype(F32) + back2[h].astype(F32) + back3[h].astype(F32)
        near = jnp.concatenate([near[:d], near[d:] + came], axis=0).astype(BF16)
        total = grads[h] + nn(near, place_matrix(tokens, count, sc[h]))
        place = one_hot(iota((8, tokens), 1) == iota((8, tokens), 0) * 64 + sc[heads + h])
        total = total + tn(far[h].astype(BF16), place)[: 3 * d]
        total = total.astype(BF16)
        for slot in range(3):
            turned[slot, h * d : (h + 1) * d, :] = total[slot * d : (slot + 1) * d]
    for slot, ref in enumerate((dq, dk, dv)):
        ref[...] = turned[slot].T


def call(kernel, name, operands, outs, scratch=(), scalars=None, flops=0):
    specs = [pl.BlockSpec(memory_space=pltpu.VMEM)] * len(operands)
    if scalars is not None:
        specs = [pl.BlockSpec(memory_space=pltpu.SMEM)] + specs
        operands = [scalars, *operands]
    size = sum(math.prod(x.shape) * x.dtype.itemsize for x in [*operands, *outs])
    return pl.pallas_call(
        kernel,
        name=name,
        out_shape=outs,
        in_specs=specs,
        out_specs=[pl.BlockSpec(memory_space=pltpu.VMEM)] * len(outs),
        scratch_shapes=list(scratch),
        compiler_params=pltpu.CompilerParams(vmem_limit_bytes=40 * 1024 * 1024),
        cost_estimate=pl.CostEstimate(flops=flops, bytes_accessed=size, transcendentals=0),
    )(*operands)


def on_device(query_rows, key_rows, value_rows, out_weight, cotangent, offsets):
    tokens, width = query_rows.shape
    heads = offsets.shape[1]
    d = width // heads
    scale = 1.0 / math.sqrt(d)
    factor = scale * LOG2E
    seq_size = lax.axis_size("seq")
    seq = lax.axis_index("seq")
    head = lax.axis_index("head")
    count = tokens // NEAR
    groups = seq_size // heads
    columns = [[a * heads + z for z in range(heads)] for a in range(groups)]

    def struct(shape, dtype):
        return jax.ShapeDtypeStruct(shape, dtype)

    extras = jnp.stack([seq % NEAR, seq // heads, head]).astype(jnp.int32)
    sc = jnp.concatenate([offsets.reshape(2 * heads), extras])

    c2 = lax.ppermute(cotangent, "head", [(i, i ^ 2) for i in range(4)])
    c1 = lax.ppermute(cotangent, "head", [(i, i ^ 1) for i in range(4)])
    c3 = lax.ppermute(c2, "head", [(i, i ^ 1) for i in range(4)])

    qkvt, near_q, near_kv, far_msg = call(
        functools.partial(prep_kernel, heads),
        "prep",
        [query_rows, key_rows, value_rows],
        [
            struct((heads, 256, tokens), BF16),
            struct((heads, d, count), BF16),
            struct((heads, 2 * d, count), BF16),
            struct((groups, heads, 16, 128), BF16),
        ],
        scalars=sc,
        flops=3_000_000_000,
    )
    far_got = lax.all_to_all(
        far_msg.reshape(seq_size, 16, 128), "seq", 0, 0, tiled=True
    )

    def shifted(x, distance):
        if distance > 0:
            route = [(i - distance, i) for i in range(seq_size) if i % NEAR >= distance]
        else:
            route = [(i, i + distance) for i in range(seq_size) if i % NEAR >= -distance]
        return lax.ppermute(x, "seq", route)

    kvs = [near_kv] + [shifted(near_kv, distance) for distance in (1, 2, 3)]
    l_out, l_norm = call(
        functools.partial(local_kernel, heads, d, factor),
        "local_forward",
        [qkvt],
        [struct((heads, d, tokens), F32), struct((heads, tokens), F32)],
        flops=5_000_000_000,
    )
    n_out, n_norm = call(
        functools.partial(near_forward_kernel, heads, d, factor),
        "near_forward",
        [near_q, *kvs],
        [struct((heads, d, count), BF16), struct((heads, count), F32)],
        scalars=sc,
        flops=2_000_000_000,
    )
    gt, out, norm, stat_msg = call(
        functools.partial(mix_kernel, heads, d),
        "mix",
        [out_weight, cotangent, c1, c2, c3, l_out, l_norm, n_out, n_norm],
        [
            struct((width, tokens), BF16),
            struct((heads, d, tokens), F32),
            struct((heads, tokens), F32),
            struct((groups, heads, 8, 128), F32),
        ],
        scalars=sc,
        flops=4_000_000_000,
    )
    stat_got = lax.all_to_all(stat_msg.reshape(seq_size, 8, 128), "seq", 0, 0, tiled=True)
    far_qkvt, far_out, far_norm, out_msg = call(
        functools.partial(far_forward_kernel, d, factor),
        "far_forward",
        [far_got],
        [
            struct((256, tokens), BF16),
            struct((d, tokens), F32),
            struct((8, tokens), F32),
            struct((64, 128), F32),
        ],
        scratch=[pltpu.VMEM((tokens, 128), F32)],
        scalars=sc,
        flops=2_000_000_000,
    )
    out_got = lax.all_to_all(
        out_msg.reshape(heads, 8, 128), "seq", 0, 0, tiled=True, axis_index_groups=columns
    )
    attended, all_norm, all_delta, own, back1, back2, back3 = call(
        functools.partial(total_kernel, heads, d, factor, scale),
        "total",
        [gt, out, norm, out_got, near_q, *kvs],
        [
            struct((tokens, width), BF16),
            struct((heads, tokens), F32),
            struct((heads, tokens), F32),
            struct((heads, 3 * d, count), BF16),
            struct((heads, 2 * d, count), BF16),
            struct((heads, 2 * d, count), BF16),
            struct((heads, 2 * d, count), BF16),
        ],
        scratch=[pltpu.VMEM((width, tokens), BF16)],
        scalars=sc,
        flops=5_000_000_000,
    )
    backs = [shifted(x, -distance) for distance, x in ((1, back1), (2, back2), (3, back3))]
    (grad_msg,) = call(
        functools.partial(far_backward_kernel, d, factor, scale),
        "far_backward",
        [far_qkvt, far_out, far_norm, stat_got],
        [struct((64, 256), F32)],
        scratch=[pltpu.VMEM((tokens, 256), F32)],
        scalars=sc,
        flops=2_000_000_000,
    )
    grad_got = lax.all_to_all(
        grad_msg.reshape(heads, 8, 256), "seq", 0, 0, tiled=True, axis_index_groups=columns
    )
    (grads,) = call(
        functools.partial(local_backward_kernel, heads, d, factor, scale),
        "local_backward",
        [qkvt, gt, all_norm, all_delta],
        [struct((heads, 3 * d, tokens), F32)],
        flops=8_000_000_000,
    )
    grad_query, grad_key, grad_value = call(
        functools.partial(final_kernel, heads, d),
        "final",
        [grads, own, *backs, grad_got],
        [struct((tokens, width), BF16)] * 3,
        scratch=[pltpu.VMEM((3, width, tokens), BF16)],
        scalars=sc,
        flops=2_000_000_000,
    )
    return (attended, grad_query, grad_key, grad_value)


def solution(mesh):
    return jax.shard_map(
        on_device,
        mesh=mesh,
        in_specs=(
            P("seq", "head"),
            P("seq", "head"),
            P("seq", "head"),
            P("head", None),
            P("seq", "head"),
            P(None, "head"),
        ),
        out_specs=(P("seq", "head"), P("seq", "head"), P("seq", "head"), P("seq", "head")),
        check_vma=False,
    )
```

```python
import functools
import math

import jax
import jax.numpy as jnp
from jax import lax
from jax.experimental import pallas as pl
from jax.experimental.pallas import tpu as pltpu
from jax.sharding import PartitionSpec as P

NEAR = 4
F32 = jnp.float32
BF16 = jnp.bfloat16
LOG2E = math.log2(math.e)
NEG = float("-inf")


def nn(a, b):
    return lax.dot_general(a, b, (((1,), (0,)), ((), ())), preferred_element_type=F32)


def nt(a, b):
    return lax.dot_general(a, b, (((1,), (1,)), ((), ())), preferred_element_type=F32)


def tn(a, b):
    return lax.dot_general(a, b, (((0,), (0,)), ((), ())), preferred_element_type=F32)


def iota(shape, dim):
    return lax.broadcasted_iota(jnp.int32, shape, dim)


def one_hot(mask):
    return jnp.where(mask, 1.0, 0.0).astype(BF16)


def pick_matrix(tokens, count, offset):
    rate = tokens // count
    return one_hot(iota((tokens, count), 0) == iota((tokens, count), 1) * rate + offset)


def place_matrix(tokens, count, offset, rows=None):
    rate = tokens // count
    rows = rows or count
    return one_hot(iota((rows, tokens), 1) == iota((rows, tokens), 0) * rate + offset)


def split3(x):
    high = x.astype(BF16).astype(F32)
    rest = x - high
    middle = rest.astype(BF16).astype(F32)
    return high, middle, rest - middle


def log2_add(a, b):
    top = jnp.maximum(a, b)
    return top + jnp.log(jnp.exp2(a - top) + jnp.exp2(b - top)) * LOG2E


def causal_mask(size):
    return iota((size, size), 0) <= iota((size, size), 1)


def halves(tokens):
    half = tokens // 2
    return half, ((0, slice(0, half)), (1, slice(half, tokens)))


def forward(qt, kt, vt, factor, diag):
    tokens = qt.shape[1]
    half, blocks = halves(tokens)
    outs, norms = [], []
    for index, cols in blocks:
        keys = (index + 1) * half
        scores = tn(kt[:, :keys], qt[:, cols])
        last = jnp.where(diag, scores[keys - half :], NEG)
        parts = [last] if index == 0 else [scores[:half], last]
        top = functools.reduce(
            jnp.maximum, [jnp.max(part, axis=0, keepdims=True) for part in parts]
        )
        top = top * factor
        probs = [jnp.exp2(part * factor - top) for part in parts]
        total = sum(jnp.sum(part, axis=0, keepdims=True) for part in probs)
        packed = [part.astype(BF16) for part in probs]
        packed = packed[0] if index == 0 else jnp.concatenate(packed, axis=0)
        outs.append(nn(vt[:, :keys], packed) / total)
        norms.append(top + jnp.log(total) * LOG2E)
    return jnp.concatenate(outs, axis=1), jnp.concatenate(norms, axis=1)


def backward(qt, kt, vt, gt, norm, delta, factor, scale, diag):
    tokens = qt.shape[1]
    half, blocks = halves(tokens)
    dq = []
    for index, cols in blocks:
        keys = (index + 1) * half
        scores = tn(kt[:, :keys], qt[:, cols]) * factor - norm[:, cols]
        last = jnp.where(diag, jnp.exp2(scores[keys - half :]), 0.0)
        if index == 0:
            probs = last
        else:
            probs = jnp.concatenate([jnp.exp2(scores[:half]), last], axis=0)
        dprobs = tn(vt[:, :keys], gt[:, cols])
        dscores = (probs * (dprobs - delta[:, cols])).astype(BF16)
        dq.append(nn(kt[:, :keys], dscores) * scale)
        dk_part = nt(qt[:, cols], dscores) * scale
        dv_part = nt(gt[:, cols], probs.astype(BF16))
        if index == 0:
            dk, dv = dk_part, dv_part
        else:
            dk = jnp.concatenate([dk + dk_part[:, :half], dk_part[:, half:]], axis=1)
            dv = jnp.concatenate([dv + dv_part[:, :half], dv_part[:, half:]], axis=1)
    return jnp.concatenate(dq, axis=1), dk, dv


def fetch(src, dst, sem):
    copy = pltpu.make_async_copy(src, dst, sem)
    copy.start()
    return copy


def both_halves(pairs, sems, size):
    return [
        [
            fetch(src.at[pl.ds(i * size, size)], dst.at[pl.ds(i * size, size)], sems.at[i, j])
            for j, (src, dst) in enumerate(pairs)
        ]
        for i in range(2)
    ]


def wait_all(copies):
    for copy in copies:
        copy.wait()


def my_offsets(offsets, heads):
    mine = lax.axis_index("seq") % heads
    return offsets[0, mine], offsets[1, mine]


def sum3(x, first, axis):
    if axis == 0:
        return x[first : first + 1] + x[first + 1 : first + 2] + x[first + 2 : first + 3]
    return x[:, first : first + 1] + x[:, first + 1 : first + 2] + x[:, first + 2 : first + 3]


def local_kernel(
    heads, factor, offsets, q, k, v, qkvt, msg, out, norm, raw, turned, res, sems, out_sems
):
    tokens, width = q.shape
    d = width // heads
    loads = [fetch(ref, raw.at[i], sems.at[i]) for i, ref in enumerate((q, k, v))]
    stores = []
    for slot in range(3):
        loads[slot].wait()
        turned[slot] = raw[slot].T
        stores.append(fetch(turned.at[slot], qkvt.at[slot], out_sems.at[slot]))
    diag = causal_mask(tokens // 2)
    for h in range(heads):
        rows = slice(h * d, (h + 1) * d)
        block = jnp.concatenate([turned[0, rows], turned[1, rows], turned[2, rows]], axis=0)
        near = nn(block, pick_matrix(tokens, tokens // NEAR, offsets[0, h]))
        msg[h, : 3 * d] = near.astype(BF16)
        picked = nt(place_matrix(tokens, 8, offsets[1, h], 16), block)[:8]
        tail = jnp.concatenate([picked[:, 128:], jnp.zeros((8, 256 - 3 * d), F32)], axis=1)
        msg[h, 3 * d :] = jnp.concatenate([picked[:, :128], tail], axis=0).astype(BF16)
        o, n = forward(block[:d], block[d : 2 * d], block[2 * d :], factor, diag)
        res[rows] = o.astype(BF16)
        norm[h : h + 1, :] = n
    stores.append(fetch(res, out, out_sems.at[3]))
    wait_all(stores)


def stats_kernel(
    heads, d, offsets, w, c0, c1, c2, c3, l_out, l_norm, gt, msg,
    w_buf, c_buf, l_buf, g_buf, sems, out_sems,
):
    tokens, width = c0.shape
    count = tokens // NEAR
    head = lax.axis_index("head")
    loads = []
    for flip, ref in enumerate((c0, c1, c2, c3)):
        first = pl.multiple_of(jnp.bitwise_xor(head, flip) * width, 128)
        loads.append(fetch(w.at[:, pl.ds(first, width)], w_buf.at[flip], sems.at[flip]))
        loads.append(fetch(ref, c_buf.at[flip], sems.at[4 + flip]))
    loads.append(fetch(l_out, l_buf, sems.at[8]))
    wait_all(loads[:4])
    grads = nt(w_buf[0], c_buf[0]) + nt(w_buf[1], c_buf[1])
    wait_all(loads[4:])
    grads = grads + nt(w_buf[2], c_buf[2]) + nt(w_buf[3], c_buf[3])
    grads = grads.astype(BF16)
    g_buf[...] = grads
    store = fetch(g_buf, gt, out_sems.at[0])
    for h in range(heads):
        rows = slice(h * d, (h + 1) * d)
        g = grads[rows].astype(F32)
        product = jnp.sum(g * l_buf[rows].astype(F32), axis=0, keepdims=True)
        stack = jnp.concatenate(
            [
                g,
                *split3(l_norm[h : h + 1, :]),
                *split3(product),
                jnp.zeros((122 - d, tokens), F32),
            ],
            axis=0,
        ).astype(BF16)
        near = nn(stack[:96], pick_matrix(tokens, count, offsets[0, h]))
        far = nt(place_matrix(tokens, 8, offsets[1, h], 16), stack)
        msg[h] = jnp.concatenate([near, far], axis=0).astype(BF16)
    store.wait()


def segment(got, first, size, part):
    pieces = [got[4 * part + z, first : first + size, :] for z in range(NEAR)]
    return jnp.concatenate(pieces, axis=1)


def near_forward_kernel(d, factor, got, msg, norm):
    tokens = NEAR * got.shape[2]
    diag = causal_mask(tokens // 2)
    for part in range(2):
        qt, kt, vt = [segment(got, i * d, d, part) for i in range(3)]
        o, n = forward(qt, kt, vt, factor, diag)
        norm[part : part + 1, :] = n
        gap = jnp.zeros((6, tokens), F32)
        rest = jnp.zeros((87 - d, tokens), F32)
        stack = jnp.concatenate([o, gap, *split3(n), rest], axis=0).astype(BF16)
        for z in range(NEAR):
            msg[4 * part + z] = stack[:, z * 128 : (z + 1) * 128]


def far_block(got):
    rows = got[...].astype(F32)
    tokens = rows.shape[0] * 8
    wide = jnp.concatenate(
        [rows[:, :8].reshape(tokens, 128), rows[:, 8:].reshape(tokens, 128)], axis=1
    )
    return wide.T.astype(BF16)


def column_rows():
    return pl.ds(pl.multiple_of(lax.axis_index("seq") // 8 * 64, 64), 64)


def far_forward_kernel(d, factor, got, stats, near, norm, msg, turned):
    block = far_block(got)
    tokens = block.shape[1]
    diag = causal_mask(tokens // 2)
    o, n = forward(block[:d], block[d : 2 * d], block[2 * d : 3 * d], factor, diag)
    norm[...] = jnp.broadcast_to(n, norm.shape)
    stack = jnp.concatenate([o, *split3(n), jnp.zeros((125 - d, tokens), F32)], axis=0)
    turned[...] = stack.T
    mine = turned[column_rows(), :].reshape(8, 8, 128)
    msg[:, :d] = stats[:, :d]
    msg[:, d : 2 * d] = near[:, :d]
    both = stats[:, d : d + 16].astype(F32) + near[:, d:].astype(F32)
    msg[:, 2 * d : 2 * d + 16] = both.astype(BF16)
    far = stats[:, d + 16 :].astype(F32)[:, :8]
    msg[:, 2 * d + 16 :] = jnp.concatenate([far, mine], axis=1).astype(BF16)


def overlap(near_offset, far_offset):
    shift = far_offset - near_offset
    spot = iota((8, 128), 0) * 16 + lax.shift_right_arithmetic(shift, 2)
    return (iota((8, 128), 1) == spot) & (lax.bitwise_and(shift, 3) == 0)


def near_stats(d, stats, outs, part):
    g = segment(stats, 0, d, part).astype(F32)
    rest = segment(stats, 2 * d, 16, part).astype(F32)
    o = segment(outs, d, d, part).astype(F32)
    product = jnp.sum(g * o, axis=0, keepdims=True)
    return g, sum3(rest, 0, 0), sum3(rest, 3, 0), product


def owner_stats_kernel(heads, d, offsets, stats, outs, near_norm, msg):
    near_offset, far_offset = my_offsets(offsets, heads)
    same = overlap(near_offset, far_offset)
    hit = jnp.max(jnp.where(same, 1.0, 0.0), axis=1, keepdims=True) > 0.5
    lane = iota((8, 128), 1)
    for part in range(2):
        _, _, _, product = near_stats(d, stats, outs, part)
        for z in range(NEAR):
            cols = slice(z * 128, (z + 1) * 128)
            near_log = near_norm[part : part + 1, cols]
            near_log = jnp.sum(jnp.where(same, near_log, 0.0), axis=1, keepdims=True)
            near_log = jnp.where(hit, near_log, NEG)
            near_dot = jnp.sum(jnp.where(same, product[:, cols], 0.0), axis=1, keepdims=True)
            rows = stats[4 * part + z, 2 * d + 16 :, :].astype(F32)[:8]
            mine = sum3(rows, d, 1)
            both = log2_add(mine, near_log)
            dot = jnp.exp2(mine - both) * sum3(rows, d + 3, 1)
            dot = dot + jnp.exp2(near_log - both) * near_dot
            for i, term in enumerate([*split3(both), *split3(dot)]):
                rows = jnp.where(lane == d + i, term, rows)
            rows = jnp.concatenate([rows, jnp.zeros_like(rows)], axis=0).astype(BF16)
            for copy in range(msg.shape[0]):
                msg[copy, 4 * part + z] = rows


def near_backward_kernel(heads, d, factor, scale, offsets, got, stats, outs, near_norm, msg):
    near_offset, far_offset = my_offsets(offsets, heads)
    same = overlap(near_offset, far_offset)
    hit = jnp.max(jnp.where(same, 1.0, 0.0), axis=0, keepdims=True) > 0.5
    tokens = near_norm.shape[1]
    diag = causal_mask(tokens // 2)
    for part in range(2):
        g, local_norm, local_dot, near_dot = near_stats(d, stats, outs, part)
        far_norms, far_dots = [], []
        for z in range(NEAR):
            rows = outs[4 * part + z, 2 * d + 16 :, :].astype(F32)[8:]
            grads = stats[4 * part + z, 2 * d + 16 :, :].astype(F32)[:8]
            dot = jnp.sum(jnp.where(iota((8, 128), 1) < d, rows * grads, 0.0), axis=1, keepdims=True)
            log = jnp.sum(jnp.where(same, sum3(rows, d, 1), 0.0), axis=0, keepdims=True)
            far_norms.append(jnp.where(hit, log, NEG))
            far_dots.append(jnp.sum(jnp.where(same, dot, 0.0), axis=0, keepdims=True))
        far_norm = jnp.concatenate(far_norms, axis=1)
        far_dot = jnp.concatenate(far_dots, axis=1)
        mine = near_norm[part : part + 1, :]
        norm = log2_add(log2_add(mine, local_norm), far_norm)
        delta = jnp.exp2(mine - norm) * near_dot + jnp.exp2(local_norm - norm) * local_dot
        delta = delta + jnp.exp2(far_norm - norm) * far_dot
        qt, kt, vt = [segment(got, i * d, d, part) for i in range(3)]
        grads = backward(qt, kt, vt, g.astype(BF16), norm, delta, factor, scale, diag)
        for slot in range(3):
            packed = grads[slot].astype(BF16)
            for z in range(NEAR):
                msg[4 * part + z, slot * d : (slot + 1) * d] = packed[:, z * 128 : (z + 1) * 128]


def far_backward_kernel(d, factor, scale, got, norm, stats, near, msg, turned):
    block = far_block(got)
    qt, kt, vt = block[:d], block[d : 2 * d], block[2 * d : 3 * d]
    tokens = block.shape[1]
    rows = stats[...].astype(F32)[:, :8].reshape(tokens, 128).T
    gt = rows[:d].astype(BF16)
    rest_norm = sum3(rows, d, 0)
    rest_dot = sum3(rows, d + 3, 0)
    mine = norm[:1, :]
    both = log2_add(mine, rest_norm)
    share = jnp.exp2(mine - both)
    rest = jnp.exp2(rest_norm - both) * rest_dot
    scores = tn(kt, qt) * factor - mine
    causal = iota((tokens, tokens), 0) <= iota((tokens, tokens), 1)
    probs = jnp.where(causal, jnp.exp2(scores), 0.0)
    dprobs = tn(vt, gt)
    delta = share * jnp.sum(probs * dprobs, axis=0, keepdims=True) + rest
    probs = probs * share
    dscores = (probs * (dprobs - delta)).astype(BF16)
    dq = nn(kt, dscores) * scale
    dk = nt(qt, dscores) * scale
    dv = nt(gt, probs.astype(BF16))
    stack = jnp.concatenate([dq, dk, dv, jnp.zeros((256 - 3 * d, tokens), F32)], axis=0)
    turned[...] = stack.T
    picked = turned[column_rows(), :]
    msg[:, : 3 * d] = near[...]
    msg[:, 3 * d :] = jnp.concatenate(
        [picked[:, :128].reshape(8, 8, 128), picked[:, 128:].reshape(8, 8, 128)], axis=1
    ).astype(BF16)


def local_backward_kernel(
    heads, d, factor, scale, offsets, qkvt, gt, l_out, l_norm, got, attended, grads,
    buf, o_buf, turned, rows_buf, sems, load_sems, out_sems,
):
    tokens = gt.shape[1]
    count = tokens // NEAR
    first = [fetch(l_out, o_buf, sems.at[0]), fetch(gt, buf.at[3], sems.at[1])]
    loads = [fetch(qkvt.at[i], buf.at[i], load_sems.at[i]) for i in range(3)]
    lane = iota((1, tokens), 1)
    diag = causal_mask(tokens // 2)
    wait_all(first)
    norms, deltas = [], []
    for h in range(heads):
        rows = slice(h * d, (h + 1) * d)
        near = nn(got[h, d : 2 * d + 16, :], place_matrix(tokens, count, offsets[0, h]))
        near_norm = jnp.where(lane % NEAR == offsets[0, h], sum3(near, d + 6, 0), NEG)
        place = iota((8, tokens), 1) == iota((8, tokens), 0) * 64 + offsets[1, h]
        came = got[h, 2 * d + 16 :, :].astype(F32)[8:]
        spread = jnp.sum(jnp.where(place, sum3(came, d, 1), 0.0), axis=0, keepdims=True)
        far_norm = jnp.where(lane % 64 == offsets[1, h], spread, NEG)
        far_out = tn(came[:, :d].astype(BF16), one_hot(place))
        mine = l_norm[h : h + 1, :]
        both = log2_add(log2_add(mine, near_norm), far_norm)
        mixed = jnp.exp2(mine - both) * o_buf[rows].astype(F32)
        mixed = mixed + jnp.exp2(near_norm - both) * near[:d]
        mixed = (mixed + jnp.exp2(far_norm - both) * far_out).astype(BF16)
        turned[rows, :] = mixed
        delta = buf[3, rows].astype(F32) * mixed.astype(F32)
        norms.append(both)
        deltas.append(jnp.sum(delta, axis=0, keepdims=True))
    rows_buf[...] = turned[...].T
    store = fetch(rows_buf, attended, out_sems.at[0])
    wait_all(loads)
    for h in range(heads):
        rows = slice(h * d, (h + 1) * d)
        parts = backward(
            buf[0, rows], buf[1, rows], buf[2, rows], buf[3, rows],
            norms[h], deltas[h], factor, scale, diag,
        )
        for slot in range(3):
            grads[slot, rows] = parts[slot].astype(grads.dtype)
    store.wait()


def final_kernel(heads, d, offsets, grads, got, dq, dk, dv, turned, rows_buf, out_sems):
    tokens = grads.shape[2]
    count = tokens // NEAR
    for h in range(heads):
        rows = slice(h * d, (h + 1) * d)
        total = nn(got[h, : 3 * d], place_matrix(tokens, count, offsets[0, h]))
        place = one_hot(iota((8, tokens), 1) == iota((8, tokens), 0) * 64 + offsets[1, h])
        far = got[h, 3 * d :].astype(F32)
        far = jnp.concatenate([far[:8], far[8:]], axis=1).astype(BF16)
        total = total + tn(far, place)[: 3 * d]
        for slot in range(3):
            mine = total[slot * d : (slot + 1) * d] + grads[slot, rows].astype(F32)
            turned[slot, rows, :] = mine.astype(BF16)
    stores = []
    for slot, ref in enumerate((dq, dk, dv)):
        rows_buf[slot] = turned[slot].T
        stores.append(fetch(rows_buf.at[slot], ref, out_sems.at[slot]))
    wait_all(stores)


def call(kernel, name, operands, outs, scratch=(), limit=63_000_000):
    spaces = {"s": pltpu.SMEM, "v": pltpu.VMEM, "h": pltpu.HBM}
    arrays = [x for x, _ in operands]
    shapes = [x for x, _ in outs]
    return pl.pallas_call(
        kernel,
        name=name,
        out_shape=shapes,
        in_specs=[pl.BlockSpec(memory_space=spaces[where]) for _, where in operands],
        out_specs=[pl.BlockSpec(memory_space=spaces[where]) for _, where in outs],
        scratch_shapes=list(scratch),
        compiler_params=pltpu.CompilerParams(vmem_limit_bytes=limit),
        cost_estimate=pl.CostEstimate(flops=1000, bytes_accessed=1000, transcendentals=0),
    )(*arrays)


def after(x, y):
    return lax.optimization_barrier((x, y))[0]


def on_device(query_rows, key_rows, value_rows, out_weight, cotangent, offsets):
    tokens, width = query_rows.shape
    heads = offsets.shape[1]
    d = width // heads
    scale = 1.0 / math.sqrt(d)
    factor = scale * LOG2E
    seq_size = lax.axis_size("seq")
    count = tokens // NEAR
    groups = seq_size // heads
    columns = [[a * heads + z for z in range(heads)] for a in range(groups)]
    planes = [[a * heads + z for a in range(groups)] for z in range(heads)]
    struct = jax.ShapeDtypeStruct
    dma = pltpu.SemaphoreType.DMA

    def vmem(*shape, dtype=BF16):
        return pltpu.VMEM(shape, dtype)

    def along_column(x):
        return lax.all_to_all(x, "seq", 0, 0, tiled=True, axis_index_groups=columns)

    def over_plane(copies):
        got = lax.all_to_all(copies, "seq", 0, 0, tiled=True, axis_index_groups=planes)
        return got.reshape(seq_size, *copies.shape[2:])

    def flipped(x, bit):
        return lax.ppermute(x, "head", [(i, i ^ bit) for i in range(4)])

    c2 = flipped(cotangent, 2)
    qkvt, rows_msg, l_out, l_norm = call(
        functools.partial(local_kernel, heads, factor),
        "local_forward",
        [(offsets, "s"), (query_rows, "h"), (key_rows, "h"), (value_rows, "h")],
        [
            (struct((3, width, tokens), BF16), "h"),
            (struct((heads, 256, count), BF16), "v"),
            (struct((width, tokens), BF16), "h"),
            (struct((heads, tokens), F32), "v"),
        ],
        scratch=[
            vmem(3, tokens, width),
            vmem(3, width, tokens),
            vmem(width, tokens),
            dma((3,)),
            dma((4,)),
        ],
    )
    rows_got = along_column(rows_msg)
    c2 = after(c2, l_norm)
    c3 = flipped(c2, 1)
    c1 = flipped(after(cotangent, l_norm), 1)
    gt, stats_msg = call(
        functools.partial(stats_kernel, heads, d),
        "stats",
        [(offsets, "s"), (out_weight, "h")]
        + [(x, "h") for x in (cotangent, c1, c2, c3)]
        + [(l_out, "h"), (l_norm, "v")],
        [
            (struct((width, tokens), BF16), "h"),
            (struct((heads, 112, 128), BF16), "v"),
        ],
        scratch=[
            vmem(4, width, width),
            vmem(4, tokens, width),
            vmem(width, tokens),
            vmem(width, tokens),
            dma((9,)),
            dma((1,)),
        ],
    )
    rows_got = after(rows_got, stats_msg)
    far_rows = rows_got[:, 3 * d :]
    far_got = over_plane(jnp.broadcast_to(far_rows[None], (groups, *far_rows.shape)))
    near_out, near_norm = call(
        functools.partial(near_forward_kernel, d, factor),
        "near_forward",
        [(rows_got, "v")],
        [(struct((heads, 96, count), BF16), "v"), (struct((2, tokens), F32), "v")],
        limit=16_000_000,
    )
    far_norm, swap_msg = call(
        functools.partial(far_forward_kernel, d, factor),
        "far_forward",
        [(far_got, "v"), (stats_msg, "v"), (near_out, "v")],
        [(struct((8, tokens), F32), "v"), (struct((heads, 192, 128), BF16), "v")],
        scratch=[vmem(tokens, 128, dtype=F32)],
        limit=16_000_000,
    )
    swap_got = along_column(swap_msg)
    (far_msg,) = call(
        functools.partial(owner_stats_kernel, heads, d),
        "owner_stats",
        [(offsets, "s"), (swap_got, "v"), (swap_msg, "v"), (near_norm, "v")],
        [(struct((groups, heads, 16, 128), BF16), "v")],
        limit=16_000_000,
    )
    far_stats = over_plane(far_msg)
    (near_msg,) = call(
        functools.partial(near_backward_kernel, heads, d, factor, scale),
        "near_backward",
        [(offsets, "s"), (rows_got, "v"), (swap_got, "v"), (swap_msg, "v"), (near_norm, "v")],
        [(struct((heads, 3 * d, count), BF16), "v")],
        limit=16_000_000,
    )
    (grad_msg,) = call(
        functools.partial(far_backward_kernel, d, factor, scale),
        "far_backward",
        [(far_got, "v"), (far_norm, "v"), (far_stats, "v"), (near_msg, "v")],
        [(struct((heads, 256, 128), BF16), "v")],
        scratch=[vmem(tokens, 256, dtype=F32)],
        limit=16_000_000,
    )
    owner_grads = along_column(grad_msg)
    swap_got = after(swap_got, grad_msg)
    attended, grads = call(
        functools.partial(local_backward_kernel, heads, d, factor, scale),
        "local_backward",
        [(offsets, "s"), (qkvt, "h"), (gt, "h"), (l_out, "h"), (l_norm, "v"), (swap_got, "v")],
        [
            (struct((tokens, width), BF16), "h"),
            (struct((3, width, tokens), BF16), "v"),
        ],
        scratch=[
            vmem(4, width, tokens),
            vmem(width, tokens),
            vmem(width, tokens),
            vmem(tokens, width),
            dma((2,)),
            dma((3,)),
            dma((1,)),
        ],
    )
    grad_query, grad_key, grad_value = call(
        functools.partial(final_kernel, heads, d),
        "final",
        [(offsets, "s"), (grads, "v"), (owner_grads, "v")],
        [(struct((tokens, width), BF16), "h")] * 3,
        scratch=[
            vmem(3, width, tokens),
            vmem(3, tokens, width),
            dma((3,)),
        ],
        limit=16_000_000,
    )
    return (attended, grad_query, grad_key, grad_value)


def solution(mesh):
    return jax.shard_map(
        on_device,
        mesh=mesh,
        in_specs=(
            P("seq", "head"),
            P("seq", "head"),
            P("seq", "head"),
            P("head", None),
            P("seq", "head"),
            P(None, "head"),
        ),
        out_specs=(P("seq", "head"), P("seq", "head"), P("seq", "head"), P("seq", "head")),
        check_vma=False,
    )
```

```python
import functools
import math

import jax
import jax.numpy as jnp
from jax import lax
from jax.experimental import pallas as pl
from jax.experimental.pallas import tpu as pltpu
from jax.sharding import PartitionSpec as P

NEAR = 4
F32 = jnp.float32
BF16 = jnp.bfloat16
LOG2E = math.log2(math.e)
NEG = float("-inf")
LOW = -1e30


def nn(a, b):
    return lax.dot_general(a, b, (((1,), (0,)), ((), ())), preferred_element_type=F32)


def nt(a, b):
    return lax.dot_general(a, b, (((1,), (1,)), ((), ())), preferred_element_type=F32)


def tn(a, b):
    return lax.dot_general(a, b, (((0,), (0,)), ((), ())), preferred_element_type=F32)


def iota(shape, dim):
    return lax.broadcasted_iota(jnp.int32, shape, dim)


def one_hot(mask):
    return jnp.where(mask, 1.0, 0.0).astype(BF16)


def pick_matrix(tokens, count, offset):
    rate = tokens // count
    return one_hot(iota((tokens, count), 0) == iota((tokens, count), 1) * rate + offset)


def place_matrix(tokens, count, offset, rows=None):
    rate = tokens // count
    rows = rows or count
    return one_hot(iota((rows, tokens), 1) == iota((rows, tokens), 0) * rate + offset)


def split3(x):
    high = x.astype(BF16).astype(F32)
    rest = x - high
    middle = rest.astype(BF16).astype(F32)
    return high, middle, rest - middle


def log2_add(a, b):
    top = jnp.maximum(a, b)
    return top + jnp.log(jnp.exp2(a - top) + jnp.exp2(b - top)) * LOG2E


def causal_mask(size):
    return iota((size, size), 0) <= iota((size, size), 1)


def halves(tokens):
    half = tokens // 2
    return half, ((0, slice(0, half)), (1, slice(half, tokens)))


def forward(qt, kt, vt, factor, diag):
    tokens = qt.shape[1]
    half, blocks = halves(tokens)
    outs, norms = [], []
    for index, cols in blocks:
        keys = (index + 1) * half
        scores = tn(kt[:, :keys], qt[:, cols])
        last = jnp.where(diag, scores[keys - half :], NEG)
        parts = [last] if index == 0 else [scores[:half], last]
        top = functools.reduce(
            jnp.maximum, [jnp.max(part, axis=0, keepdims=True) for part in parts]
        )
        top = top * factor
        probs = [jnp.exp2(part * factor - top) for part in parts]
        total = sum(jnp.sum(part, axis=0, keepdims=True) for part in probs)
        packed = [part.astype(BF16) for part in probs]
        packed = packed[0] if index == 0 else jnp.concatenate(packed, axis=0)
        outs.append(nn(vt[:, :keys], packed) / total)
        norms.append(top + jnp.log(total) * LOG2E)
    return jnp.concatenate(outs, axis=1), jnp.concatenate(norms, axis=1)


def backward(qt, kt, vt, gt, norm, delta, factor, scale, diag):
    tokens = qt.shape[1]
    half, blocks = halves(tokens)
    dq = []
    for index, cols in blocks:
        keys = (index + 1) * half
        scores = tn(kt[:, :keys], qt[:, cols]) * factor - norm[:, cols]
        last = jnp.where(diag, jnp.exp2(scores[keys - half :]), 0.0)
        if index == 0:
            probs = last
        else:
            probs = jnp.concatenate([jnp.exp2(scores[:half]), last], axis=0)
        dprobs = tn(vt[:, :keys], gt[:, cols])
        dscores = (probs * (dprobs - delta[:, cols])).astype(BF16)
        dq.append(nn(kt[:, :keys], dscores) * scale)
        dk_part = nt(qt[:, cols], dscores) * scale
        dv_part = nt(gt[:, cols], probs.astype(BF16))
        if index == 0:
            dk, dv = dk_part, dv_part
        else:
            dk = jnp.concatenate([dk + dk_part[:, :half], dk_part[:, half:]], axis=1)
            dv = jnp.concatenate([dv + dv_part[:, :half], dv_part[:, half:]], axis=1)
    return jnp.concatenate(dq, axis=1), dk, dv


def fetch(src, dst, sem):
    copy = pltpu.make_async_copy(src, dst, sem)
    copy.start()
    return copy


def both_halves(pairs, sems, size):
    return [
        [
            fetch(src.at[pl.ds(i * size, size)], dst.at[pl.ds(i * size, size)], sems.at[i, j])
            for j, (src, dst) in enumerate(pairs)
        ]
        for i in range(2)
    ]


def wait_all(copies):
    for copy in copies:
        copy.wait()


def my_offsets(offsets, heads):
    mine = lax.axis_index("seq") % heads
    return offsets[0, mine], offsets[1, mine]


def sum3(x, first, axis):
    if axis == 0:
        return x[first : first + 1] + x[first + 1 : first + 2] + x[first + 2 : first + 3]
    return x[:, first : first + 1] + x[:, first + 1 : first + 2] + x[:, first + 2 : first + 3]


def local_kernel(
    heads, factor, offsets, q, k, v, qkvt, msg, out, norm, raw, turned, sent, res, sems, out_sems
):
    tokens, width = q.shape
    d = width // heads
    loads = [fetch(ref, raw.at[i], sems.at[i]) for i, ref in enumerate((q, k, v))]
    stores = []
    for slot in range(3):
        loads[slot].wait()
        turned[slot] = raw[slot].T
        stores.append(fetch(turned.at[slot], qkvt.at[slot], out_sems.at[slot]))
    diag = causal_mask(tokens // 2)
    for h in range(heads):
        rows = slice(h * d, (h + 1) * d)
        block = jnp.concatenate([turned[0, rows], turned[1, rows], turned[2, rows]], axis=0)
        near = nn(block, pick_matrix(tokens, tokens // NEAR, offsets[0, h]))
        sent[h, : 3 * d] = near.astype(BF16)
        picked = nt(place_matrix(tokens, 8, offsets[1, h], 16), block)[:8]
        tail = jnp.concatenate([picked[:, 128:], jnp.zeros((8, 256 - 3 * d), F32)], axis=1)
        sent[h, 3 * d :] = jnp.concatenate([picked[:, :128], tail], axis=0).astype(BF16)
    stores.append(fetch(sent, msg, out_sems.at[3]))
    size = heads // 2 * d
    for part in range(2):
        for h in range(part * heads // 2, (part + 1) * heads // 2):
            rows = slice(h * d, (h + 1) * d)
            o, n = forward(turned[0, rows], turned[1, rows], turned[2, rows], factor, diag)
            res[rows] = o.astype(BF16)
            norm[h : h + 1, :] = n
        half = pl.ds(part * size, size)
        stores.append(fetch(res.at[half], out.at[half], out_sems.at[4 + part]))
    wait_all(stores)


def stats_kernel(
    heads, d, offsets, w, c0, c1, c2, c3, l_out, l_norm, gt, msg,
    w_buf, c_buf, l_buf, g_buf, sems, out_sems,
):
    tokens, width = c0.shape
    count = tokens // NEAR
    head = lax.axis_index("head")
    loads = []
    for flip, ref in enumerate((c0, c1, c2, c3)):
        first = pl.multiple_of(jnp.bitwise_xor(head, flip) * width, 128)
        loads.append(fetch(w.at[:, pl.ds(first, width)], w_buf.at[flip], sems.at[flip]))
        loads.append(fetch(ref, c_buf.at[flip], sems.at[4 + flip]))
    loads.append(fetch(l_out, l_buf, sems.at[8]))
    wait_all(loads[:4])
    grads = nt(w_buf[0], c_buf[0]) + nt(w_buf[1], c_buf[1])
    wait_all(loads[4:])
    grads = grads + nt(w_buf[2], c_buf[2]) + nt(w_buf[3], c_buf[3])
    grads = grads.astype(BF16)
    g_buf[...] = grads
    store = fetch(g_buf, gt, out_sems.at[0])
    for h in range(heads):
        rows = slice(h * d, (h + 1) * d)
        g = grads[rows].astype(F32)
        product = jnp.sum(g * l_buf[rows].astype(F32), axis=0, keepdims=True)
        stack = jnp.concatenate(
            [
                g,
                *split3(l_norm[h : h + 1, :]),
                *split3(product),
                jnp.zeros((122 - d, tokens), F32),
            ],
            axis=0,
        ).astype(BF16)
        near = nn(stack[:96], pick_matrix(tokens, count, offsets[0, h]))
        far = nt(place_matrix(tokens, 8, offsets[1, h], 16), stack)
        msg[h] = jnp.concatenate([near, far], axis=0).astype(BF16)
    store.wait()


def segment(got, first, size, part):
    pieces = [got[4 * part + z, first : first + size, :] for z in range(NEAR)]
    return jnp.concatenate(pieces, axis=1)


def overlap(near_offset, far_offset):
    shift = far_offset - near_offset
    spot = iota((8, 128), 0) * 16 + lax.shift_right_arithmetic(shift, 2)
    return (iota((8, 128), 1) == spot) & (lax.bitwise_and(shift, 3) == 0)


def near_forward_kernel(heads, d, factor, offsets, got, stats, msg, norm, shared, buf, sems):
    tokens = NEAR * got.shape[2]
    load = fetch(stats, buf, sems.at[0])
    diag = causal_mask(tokens // 2)
    same = overlap(*my_offsets(offsets, heads))
    hit = jnp.max(jnp.where(same, 1.0, 0.0), axis=1, keepdims=True) > 0.5
    twice = one_hot(jnp.concatenate([same, same], axis=0))
    lane = iota((8, 96), 1)
    stacks = []
    for part in range(2):
        qt, kt, vt = [segment(got, i * d, d, part) for i in range(3)]
        o, n = forward(qt, kt, vt, factor, diag)
        norm[part : part + 1, :] = n
        gap = jnp.zeros((6, tokens), F32)
        rest = jnp.zeros((87 - d, tokens), F32)
        stacks.append(jnp.concatenate([o, gap, *split3(n), rest], axis=0))
    load.wait()
    for part in range(2):
        for z in range(NEAR):
            spot = 4 * part + z
            piece = stacks[part][:, z * 128 : (z + 1) * 128]
            packed = piece.astype(BF16)
            msg[spot, :d] = buf[spot, :d]
            msg[spot, d : 2 * d] = packed[:d]
            both = buf[spot, d : d + 16].astype(F32) + piece[d:]
            msg[spot, 2 * d :] = both.astype(BF16)
            picked = nt(twice, packed)[:8]
            picked = jnp.where((lane == d + 6) & ~hit, LOW, picked)
            picked = jnp.concatenate([picked, jnp.zeros((8, 32), F32)], axis=1)
            rows = buf[spot, d + 16 :].astype(F32)[:8]
            rows = jnp.concatenate([picked, rows], axis=0).astype(BF16)
            for copy in range(shared.shape[0]):
                shared[copy, spot, :16] = got[spot, 3 * d :]
                shared[copy, spot, 16:] = rows


def far_block(got):
    rows = got[:, :, :16, :].astype(F32).reshape(64, 16, 128)
    wide = jnp.concatenate(
        [rows[:, :8].reshape(512, 128), rows[:, 8:].reshape(512, 128)], axis=1
    )
    return wide.T.astype(BF16)


def column_rows():
    return pl.ds(pl.multiple_of(lax.axis_index("seq") // 8 * 64, 64), 64)


def far_forward_kernel(d, factor, got, near, norm, msg, keep, turned, sems):
    copy = fetch(got, keep, sems.at[0])
    block = far_block(got)
    tokens = block.shape[1]
    diag = causal_mask(tokens // 2)
    o, n = forward(block[:d], block[d : 2 * d], block[2 * d : 3 * d], factor, diag)
    norm[...] = jnp.broadcast_to(n, norm.shape)
    stack = jnp.concatenate([o, *split3(n), jnp.zeros((125 - d, tokens), F32)], axis=0)
    turned[...] = stack.T
    mine = turned[column_rows(), :].reshape(8, 8, 128)
    msg[:, : 2 * d + 16] = near[...]
    rows = got[:, :, 16:, :].astype(F32)
    for h in range(msg.shape[0]):
        far = rows[:, h, 8:, :].reshape(64, 128)
        msg[h, 2 * d + 16 : 2 * d + 80] = far.astype(BF16)
    msg[:, 2 * d + 80 :] = jnp.concatenate([mine, jnp.zeros_like(mine)], axis=1).astype(BF16)
    copy.wait()


def near_stats(d, stats, outs, part):
    g = segment(stats, 0, d, part).astype(F32)
    rest = segment(stats, 2 * d, 16, part).astype(F32)
    o = segment(outs, d, d, part).astype(F32)
    product = jnp.sum(g * o, axis=0, keepdims=True)
    return g, sum3(rest, 0, 0), sum3(rest, 3, 0), product


def owner_backward_kernel(
    heads, d, factor, scale, offsets, got, stats, mine, outs, near_norm, kept, far_norm,
    msg, kept_buf, rows_buf, turned, sems,
):
    copy = fetch(kept, kept_buf, sems.at[0])
    rows_buf[...] = stats[:, 2 * d + 16 : 2 * d + 80].astype(F32)
    near_offset, far_offset = my_offsets(offsets, heads)
    same = overlap(near_offset, far_offset)
    hit = jnp.max(jnp.where(same, 1.0, 0.0), axis=0, keepdims=True) > 0.5
    tokens = near_norm.shape[1]
    diag = causal_mask(tokens // 2)
    plane = pl.ds(pl.multiple_of(lax.axis_index("seq") // 8 * 8, 8), 8)
    lane = iota((8, 128), 1)
    copy.wait()
    for part in range(2):
        g, local_norm, local_dot, near_dot = near_stats(d, stats, outs, part)
        far_norms, far_dots = [], []
        for z in range(NEAR):
            rows = mine[4 * part + z, 2 * d + 80 :, :].astype(F32)[:8]
            grads = rows_buf[4 * part + z, plane, :]
            dot = jnp.sum(jnp.where(lane < d, rows * grads, 0.0), axis=1, keepdims=True)
            log = jnp.sum(jnp.where(same, sum3(rows, d, 1), 0.0), axis=0, keepdims=True)
            far_norms.append(jnp.where(hit, log, NEG))
            far_dots.append(jnp.sum(jnp.where(same, dot, 0.0), axis=0, keepdims=True))
        extra = jnp.concatenate(far_norms, axis=1)
        extra_dot = jnp.concatenate(far_dots, axis=1)
        own = near_norm[part : part + 1, :]
        norm = log2_add(log2_add(own, local_norm), extra)
        delta = jnp.exp2(own - norm) * near_dot + jnp.exp2(local_norm - norm) * local_dot
        delta = delta + jnp.exp2(extra - norm) * extra_dot
        qt, kt, vt = [segment(got, i * d, d, part) for i in range(3)]
        grads = backward(qt, kt, vt, g.astype(BF16), norm, delta, factor, scale, diag)
        for slot in range(3):
            packed = grads[slot].astype(BF16)
            for z in range(NEAR):
                msg[4 * part + z, slot * d : (slot + 1) * d] = packed[:, z * 128 : (z + 1) * 128]
    block = far_block(kept_buf)
    qt, kt, vt = block[:d], block[d : 2 * d], block[2 * d : 3 * d]
    pieces = [rows_buf[z, 8 * a : 8 * a + 8, :] for a in range(8) for z in range(heads)]
    rows = jnp.concatenate(pieces, axis=0).T
    near = kept_buf[:, :, 16:, :].astype(F32)[:, :, :8, :].reshape(tokens, 128).T
    gt = rows[:d].astype(BF16)
    local_norm, other_norm = sum3(rows, d, 0), sum3(near, d + 6, 0)
    own = far_norm[:1, :]
    norm = log2_add(log2_add(own, local_norm), other_norm)
    share = jnp.exp2(own - norm)
    rest = jnp.exp2(local_norm - norm) * sum3(rows, d + 3, 0)
    other = jnp.sum(rows[:d] * near[:d], axis=0, keepdims=True)
    rest = rest + jnp.exp2(other_norm - norm) * other
    scores = tn(kt, qt) * factor - own
    causal = iota((tokens, tokens), 0) <= iota((tokens, tokens), 1)
    probs = jnp.where(causal, jnp.exp2(scores), 0.0)
    dprobs = tn(vt, gt)
    delta = share * jnp.sum(probs * dprobs, axis=0, keepdims=True) + rest
    probs = probs * share
    dscores = (probs * (dprobs - delta)).astype(BF16)
    dq = nn(kt, dscores) * scale
    dk = nt(qt, dscores) * scale
    dv = nt(gt, probs.astype(BF16))
    stack = jnp.concatenate([dq, dk, dv, jnp.zeros((256 - 3 * d, tokens), F32)], axis=0)
    turned[...] = stack.T
    picked = turned[column_rows(), :]
    msg[:, 3 * d :] = jnp.concatenate(
        [picked[:, :128].reshape(8, 8, 128), picked[:, 128:].reshape(8, 8, 128)], axis=1
    ).astype(BF16)


def local_backward_kernel(
    heads, d, factor, scale, offsets, qkvt, gt, l_out, l_norm, got, attended, grads,
    buf, o_buf, turned, rows_buf, res, sems, load_sems, out_sems,
):
    tokens = gt.shape[1]
    count = tokens // NEAR
    first = [fetch(l_out, o_buf, sems.at[0]), fetch(gt, buf.at[3], sems.at[1])]
    loads = [fetch(qkvt.at[i], buf.at[i], load_sems.at[i]) for i in range(3)]
    lane = iota((1, tokens), 1)
    diag = causal_mask(tokens // 2)
    wait_all(first)
    norms, deltas = [], []
    for h in range(heads):
        rows = slice(h * d, (h + 1) * d)
        near = nn(got[h, d : 2 * d + 16, :], place_matrix(tokens, count, offsets[0, h]))
        near_norm = jnp.where(lane % NEAR == offsets[0, h], sum3(near, d + 6, 0), NEG)
        place = iota((8, tokens), 1) == iota((8, tokens), 0) * 64 + offsets[1, h]
        came = got[h, 2 * d + 80 :, :].astype(F32)[:8]
        spread = jnp.sum(jnp.where(place, sum3(came, d, 1), 0.0), axis=0, keepdims=True)
        far_norm = jnp.where(lane % 64 == offsets[1, h], spread, NEG)
        far_out = tn(came[:, :d].astype(BF16), one_hot(place))
        mine = l_norm[h : h + 1, :]
        both = log2_add(log2_add(mine, near_norm), far_norm)
        mixed = jnp.exp2(mine - both) * o_buf[rows].astype(F32)
        mixed = mixed + jnp.exp2(near_norm - both) * near[:d]
        mixed = (mixed + jnp.exp2(far_norm - both) * far_out).astype(BF16)
        turned[rows, :] = mixed
        delta = buf[3, rows].astype(F32) * mixed.astype(F32)
        norms.append(both)
        deltas.append(jnp.sum(delta, axis=0, keepdims=True))
    rows_buf[...] = turned[...].T
    store = fetch(rows_buf, attended, out_sems.at[0])
    wait_all(loads)
    size = heads // 2 * d
    stores = [store]
    for part in range(2):
        for h in range(part * heads // 2, (part + 1) * heads // 2):
            rows = slice(h * d, (h + 1) * d)
            parts = backward(
                buf[0, rows], buf[1, rows], buf[2, rows], buf[3, rows],
                norms[h], deltas[h], factor, scale, diag,
            )
            for slot in range(3):
                res[slot, rows] = parts[slot].astype(res.dtype)
        half = pl.ds(part * size, size)
        for slot in range(3):
            stores.append(
                fetch(res.at[slot, half], grads.at[slot, half], out_sems.at[1 + 3 * part + slot])
            )
    wait_all(stores)


def final_kernel(heads, d, offsets, grads, got, dq, dk, dv, turned, rows_buf, out_sems):
    tokens = grads.shape[2]
    count = tokens // NEAR
    for h in range(heads):
        rows = slice(h * d, (h + 1) * d)
        total = nn(got[h, : 3 * d], place_matrix(tokens, count, offsets[0, h]))
        place = one_hot(iota((8, tokens), 1) == iota((8, tokens), 0) * 64 + offsets[1, h])
        far = got[h, 3 * d :].astype(F32)
        far = jnp.concatenate([far[:8], far[8:]], axis=1).astype(BF16)
        total = total + tn(far, place)[: 3 * d]
        for slot in range(3):
            mine = total[slot * d : (slot + 1) * d] + grads[slot, rows].astype(F32)
            turned[slot, rows, :] = mine.astype(BF16)
    stores = []
    for slot, ref in enumerate((dq, dk, dv)):
        rows_buf[slot] = turned[slot].T
        stores.append(fetch(rows_buf.at[slot], ref, out_sems.at[slot]))
    wait_all(stores)


def call(kernel, name, operands, outs, scratch=(), limit=63_000_000):
    spaces = {"s": pltpu.SMEM, "v": pltpu.VMEM, "h": pltpu.HBM}
    arrays = [x for x, _ in operands]
    shapes = [x for x, _ in outs]
    return pl.pallas_call(
        kernel,
        name=name,
        out_shape=shapes,
        in_specs=[pl.BlockSpec(memory_space=spaces[where]) for _, where in operands],
        out_specs=[pl.BlockSpec(memory_space=spaces[where]) for _, where in outs],
        scratch_shapes=list(scratch),
        compiler_params=pltpu.CompilerParams(vmem_limit_bytes=limit),
        cost_estimate=pl.CostEstimate(flops=1000, bytes_accessed=1000, transcendentals=0),
    )(*arrays)


def after(x, y):
    return lax.optimization_barrier((x, y))[0]


def on_device(query_rows, key_rows, value_rows, out_weight, cotangent, offsets):
    tokens, width = query_rows.shape
    heads = offsets.shape[1]
    d = width // heads
    scale = 1.0 / math.sqrt(d)
    factor = scale * LOG2E
    seq_size = lax.axis_size("seq")
    count = tokens // NEAR
    groups = seq_size // heads
    columns = [[a * heads + z for z in range(heads)] for a in range(groups)]
    planes = [[a * heads + z for a in range(groups)] for z in range(heads)]
    struct = jax.ShapeDtypeStruct
    dma = pltpu.SemaphoreType.DMA

    def vmem(*shape, dtype=BF16):
        return pltpu.VMEM(shape, dtype)

    def along_column(x):
        return lax.all_to_all(x, "seq", 0, 0, tiled=True, axis_index_groups=columns)

    def over_plane(copies):
        return lax.all_to_all(copies, "seq", 0, 0, tiled=True, axis_index_groups=planes)

    def flipped(x, bit):
        return lax.ppermute(x, "head", [(i, i ^ bit) for i in range(4)])

    c2 = flipped(cotangent, 2)
    c1 = flipped(cotangent, 1)
    qkvt, rows_msg, l_out, l_norm = call(
        functools.partial(local_kernel, heads, factor),
        "local_forward",
        [(offsets, "s"), (query_rows, "h"), (key_rows, "h"), (value_rows, "h")],
        [
            (struct((3, width, tokens), BF16), "h"),
            (struct((heads, 256, count), BF16), "h"),
            (struct((width, tokens), BF16), "h"),
            (struct((heads, tokens), F32), "v"),
        ],
        scratch=[
            vmem(3, tokens, width),
            vmem(3, width, tokens),
            vmem(heads, 256, count),
            vmem(width, tokens),
            dma((3,)),
            dma((6,)),
        ],
    )
    rows_got = along_column(rows_msg)
    c2 = after(c2, l_norm)
    c3 = flipped(c2, 1)
    gt, stats_msg = call(
        functools.partial(stats_kernel, heads, d),
        "stats",
        [(offsets, "s"), (out_weight, "h")]
        + [(x, "h") for x in (cotangent, c1, c2, c3)]
        + [(l_out, "h"), (l_norm, "v")],
        [
            (struct((width, tokens), BF16), "h"),
            (struct((heads, 112, 128), BF16), "v"),
        ],
        scratch=[
            vmem(4, width, width),
            vmem(4, tokens, width),
            vmem(width, tokens),
            vmem(width, tokens),
            dma((9,)),
            dma((1,)),
        ],
    )
    rows_got = after(rows_got, stats_msg)
    near_out, near_norm, shared = call(
        functools.partial(near_forward_kernel, heads, d, factor),
        "near_forward",
        [(offsets, "s"), (rows_got, "v"), (stats_msg, "h")],
        [
            (struct((heads, 176, count), BF16), "v"),
            (struct((2, tokens), F32), "v"),
            (struct((groups, heads, 32, 128), BF16), "v"),
        ],
        scratch=[vmem(heads, 112, 128), dma((1,))],
        limit=16_000_000,
    )
    far_got = over_plane(shared)
    far_norm, swap_msg, far_kept = call(
        functools.partial(far_forward_kernel, d, factor),
        "far_forward",
        [(far_got, "v"), (near_out, "v")],
        [
            (struct((8, tokens), F32), "v"),
            (struct((heads, 256, 128), BF16), "v"),
            (struct((groups, heads, 32, 128), BF16), "h"),
        ],
        scratch=[vmem(tokens, 128, dtype=F32), dma((1,))],
        limit=16_000_000,
    )
    swap_got = along_column(swap_msg)
    (grad_msg,) = call(
        functools.partial(owner_backward_kernel, heads, d, factor, scale),
        "owner_backward",
        [(offsets, "s"), (rows_got, "v"), (swap_got, "v"), (swap_msg, "v"), (near_out, "v")]
        + [(near_norm, "v"), (far_kept, "h"), (far_norm, "v")],
        [(struct((heads, 256, 128), BF16), "v")],
        scratch=[
            vmem(groups, heads, 32, 128),
            vmem(heads, 64, 128, dtype=F32),
            vmem(tokens, 256, dtype=F32),
            dma((1,)),
        ],
        limit=16_000_000,
    )
    owner_grads = along_column(grad_msg)
    swap_got = after(swap_got, grad_msg)
    attended, grads = call(
        functools.partial(local_backward_kernel, heads, d, factor, scale),
        "local_backward",
        [(offsets, "s"), (qkvt, "h"), (gt, "h"), (l_out, "h"), (l_norm, "v"), (swap_got, "v")],
        [
            (struct((tokens, width), BF16), "h"),
            (struct((3, width, tokens), BF16), "h"),
        ],
        scratch=[
            vmem(4, width, tokens),
            vmem(width, tokens),
            vmem(width, tokens),
            vmem(tokens, width),
            vmem(3, width, tokens),
            dma((2,)),
            dma((3,)),
            dma((7,)),
        ],
    )
    grad_query, grad_key, grad_value = call(
        functools.partial(final_kernel, heads, d),
        "final",
        [(offsets, "s"), (grads, "v"), (owner_grads, "v")],
        [(struct((tokens, width), BF16), "h")] * 3,
        scratch=[
            vmem(3, width, tokens),
            vmem(3, tokens, width),
            dma((3,)),
        ],
        limit=16_000_000,
    )
    return (attended, grad_query, grad_key, grad_value)


def solution(mesh):
    return jax.shard_map(
        on_device,
        mesh=mesh,
        in_specs=(
            P("seq", "head"),
            P("seq", "head"),
            P("seq", "head"),
            P("head", None),
            P("seq", "head"),
            P(None, "head"),
        ),
        out_specs=(P("seq", "head"), P("seq", "head"), P("seq", "head"), P("seq", "head")),
        check_vma=False,
    )
```

```python
import functools
import math

import jax
import jax.numpy as jnp
from jax import lax
from jax.experimental import pallas as pl
from jax.experimental.pallas import tpu as pltpu
from jax.sharding import PartitionSpec as P

NEAR = 4
F32 = jnp.float32
BF16 = jnp.bfloat16
LOG2E = math.log2(math.e)
NEG = float("-inf")
LOW = -1e30


def nn(a, b):
    return lax.dot_general(a, b, (((1,), (0,)), ((), ())), preferred_element_type=F32)


def nt(a, b):
    return lax.dot_general(a, b, (((1,), (1,)), ((), ())), preferred_element_type=F32)


def tn(a, b):
    return lax.dot_general(a, b, (((0,), (0,)), ((), ())), preferred_element_type=F32)


def iota(shape, dim):
    return lax.broadcasted_iota(jnp.int32, shape, dim)


def one_hot(mask):
    return jnp.where(mask, 1.0, 0.0).astype(BF16)


def pick_matrix(tokens, count, offset):
    rate = tokens // count
    return one_hot(iota((tokens, count), 0) == iota((tokens, count), 1) * rate + offset)


def place_matrix(tokens, count, offset, rows=None):
    rate = tokens // count
    rows = rows or count
    return one_hot(iota((rows, tokens), 1) == iota((rows, tokens), 0) * rate + offset)


def split3(x):
    high = x.astype(BF16).astype(F32)
    rest = x - high
    middle = rest.astype(BF16).astype(F32)
    return high, middle, rest - middle


def log2_add(a, b):
    top = jnp.maximum(a, b)
    return top + jnp.log(jnp.exp2(a - top) + jnp.exp2(b - top)) * LOG2E


def causal_mask(size):
    return iota((size, size), 0) <= iota((size, size), 1)


def halves(tokens):
    half = tokens // 2
    return half, ((0, slice(0, half)), (1, slice(half, tokens)))


def forward(qt, kt, vt, factor, diag):
    tokens = qt.shape[1]
    half, blocks = halves(tokens)
    outs, norms = [], []
    for index, cols in blocks:
        keys = (index + 1) * half
        scores = tn(kt[:, :keys], qt[:, cols])
        last = jnp.where(diag, scores[keys - half :], NEG)
        parts = [last] if index == 0 else [scores[:half], last]
        top = functools.reduce(
            jnp.maximum, [jnp.max(part, axis=0, keepdims=True) for part in parts]
        )
        top = top * factor
        probs = [jnp.exp2(part * factor - top) for part in parts]
        total = sum(jnp.sum(part, axis=0, keepdims=True) for part in probs)
        packed = [part.astype(BF16) for part in probs]
        packed = packed[0] if index == 0 else jnp.concatenate(packed, axis=0)
        outs.append(nn(vt[:, :keys], packed) / total)
        norms.append(top + jnp.log(total) * LOG2E)
    return jnp.concatenate(outs, axis=1), jnp.concatenate(norms, axis=1)


def backward(qt, kt, vt, gt, norm, delta, factor, scale, diag, share=None):
    tokens = qt.shape[1]
    half, blocks = halves(tokens)
    dq = []
    for index, cols in blocks:
        keys = (index + 1) * half
        scores = tn(kt[:, :keys], qt[:, cols]) * factor - norm[:, cols]
        last = jnp.where(diag, jnp.exp2(scores[keys - half :]), 0.0)
        if index == 0:
            probs = last
        else:
            probs = jnp.concatenate([jnp.exp2(scores[:half]), last], axis=0)
        dprobs = tn(vt[:, :keys], gt[:, cols])
        total = delta[:, cols]
        if share is not None:
            mine = jnp.sum(probs * dprobs, axis=0, keepdims=True)
            total = total + share[:, cols] * mine
            probs = probs * share[:, cols]
        dscores = (probs * (dprobs - total)).astype(BF16)
        dq.append(nn(kt[:, :keys], dscores) * scale)
        dk_part = nt(qt[:, cols], dscores) * scale
        dv_part = nt(gt[:, cols], probs.astype(BF16))
        if index == 0:
            dk, dv = dk_part, dv_part
        else:
            dk = jnp.concatenate([dk + dk_part[:, :half], dk_part[:, half:]], axis=1)
            dv = jnp.concatenate([dv + dv_part[:, :half], dv_part[:, half:]], axis=1)
    return jnp.concatenate(dq, axis=1), dk, dv


def fetch(src, dst, sem):
    copy = pltpu.make_async_copy(src, dst, sem)
    copy.start()
    return copy


def both_halves(pairs, sems, size):
    return [
        [
            fetch(src.at[pl.ds(i * size, size)], dst.at[pl.ds(i * size, size)], sems.at[i, j])
            for j, (src, dst) in enumerate(pairs)
        ]
        for i in range(2)
    ]


def wait_all(copies):
    for copy in copies:
        copy.wait()


def my_offsets(offsets, heads):
    mine = lax.axis_index("seq") % heads
    return offsets[0, mine], offsets[1, mine]


def sum3(x, first, axis):
    if axis == 0:
        return x[first : first + 1] + x[first + 1 : first + 2] + x[first + 2 : first + 3]
    return x[:, first : first + 1] + x[:, first + 1 : first + 2] + x[:, first + 2 : first + 3]


def local_kernel(
    heads, factor, offsets, q, k, v, qkvt, msg, out, norm, raw, turned, sent, res, sems, out_sems
):
    tokens, width = q.shape
    d = width // heads
    loads = [fetch(ref, raw.at[i], sems.at[i]) for i, ref in enumerate((q, k, v))]
    stores = []
    for slot in range(3):
        loads[slot].wait()
        turned[slot] = raw[slot].T
        stores.append(fetch(turned.at[slot], qkvt.at[slot], out_sems.at[slot]))
    diag = causal_mask(tokens // 2)
    for h in range(heads):
        rows = slice(h * d, (h + 1) * d)
        block = jnp.concatenate([turned[0, rows], turned[1, rows], turned[2, rows]], axis=0)
        near = nn(block, pick_matrix(tokens, tokens // NEAR, offsets[0, h]))
        sent[h, : 3 * d] = near.astype(BF16)
        picked = nt(place_matrix(tokens, 8, offsets[1, h], 16), block)[:8]
        tail = jnp.concatenate([picked[:, 128:], jnp.zeros((8, 256 - 3 * d), F32)], axis=1)
        sent[h, 3 * d :] = jnp.concatenate([picked[:, :128], tail], axis=0).astype(BF16)
    stores.append(fetch(sent, msg, out_sems.at[3]))
    size = heads // 2 * d
    for part in range(2):
        for h in range(part * heads // 2, (part + 1) * heads // 2):
            rows = slice(h * d, (h + 1) * d)
            o, n = forward(turned[0, rows], turned[1, rows], turned[2, rows], factor, diag)
            res[rows] = o.astype(BF16)
            norm[h : h + 1, :] = n
        half = pl.ds(part * size, size)
        stores.append(fetch(res.at[half], out.at[half], out_sems.at[4 + part]))
    wait_all(stores)


def stats_kernel(
    heads, d, offsets, w, c0, c1, c2, c3, l_out, l_norm, gt, msg,
    w_buf, c_buf, l_buf, g_buf, sems, out_sems,
):
    tokens, width = c0.shape
    count = tokens // NEAR
    head = lax.axis_index("head")
    loads = []
    for flip, ref in enumerate((c0, c1, c2, c3)):
        first = pl.multiple_of(jnp.bitwise_xor(head, flip) * width, 128)
        loads.append(fetch(w.at[:, pl.ds(first, width)], w_buf.at[flip], sems.at[flip]))
        loads.append(fetch(ref, c_buf.at[flip], sems.at[4 + flip]))
    loads.append(fetch(l_out, l_buf, sems.at[8]))
    wait_all(loads[:4])
    grads = nt(w_buf[0], c_buf[0]) + nt(w_buf[1], c_buf[1])
    wait_all(loads[4:])
    grads = grads + nt(w_buf[2], c_buf[2]) + nt(w_buf[3], c_buf[3])
    grads = grads.astype(BF16)
    g_buf[...] = grads
    store = fetch(g_buf, gt, out_sems.at[0])
    for h in range(heads):
        rows = slice(h * d, (h + 1) * d)
        g = grads[rows].astype(F32)
        product = jnp.sum(g * l_buf[rows].astype(F32), axis=0, keepdims=True)
        stack = jnp.concatenate(
            [
                g,
                *split3(l_norm[h : h + 1, :]),
                *split3(product),
                jnp.zeros((122 - d, tokens), F32),
            ],
            axis=0,
        ).astype(BF16)
        near = nn(stack[:96], pick_matrix(tokens, count, offsets[0, h]))
        far = nt(place_matrix(tokens, 8, offsets[1, h], 16), stack)
        msg[h] = jnp.concatenate([near, far], axis=0).astype(BF16)
    store.wait()


def segment(got, first, size, part):
    pieces = [got[4 * part + z, first : first + size, :] for z in range(NEAR)]
    return jnp.concatenate(pieces, axis=1)


def overlap(near_offset, far_offset):
    shift = far_offset - near_offset
    spot = iota((8, 128), 0) * 16 + lax.shift_right_arithmetic(shift, 2)
    return (iota((8, 128), 1) == spot) & (lax.bitwise_and(shift, 3) == 0)


def near_forward_kernel(heads, d, factor, offsets, got, stats, msg, norm, shared, buf, sems):
    tokens = NEAR * got.shape[2]
    load = fetch(stats, buf, sems.at[0])
    diag = causal_mask(tokens // 2)
    same = overlap(*my_offsets(offsets, heads))
    hit = jnp.max(jnp.where(same, 1.0, 0.0), axis=1, keepdims=True) > 0.5
    twice = one_hot(jnp.concatenate([same, same], axis=0))
    lane = iota((8, 96), 1)
    stacks = []
    for part in range(2):
        qt, kt, vt = [segment(got, i * d, d, part) for i in range(3)]
        o, n = forward(qt, kt, vt, factor, diag)
        norm[part : part + 1, :] = n
        gap = jnp.zeros((6, tokens), F32)
        rest = jnp.zeros((87 - d, tokens), F32)
        stacks.append(jnp.concatenate([o, gap, *split3(n), rest], axis=0))
    load.wait()
    for part in range(2):
        for z in range(NEAR):
            spot = 4 * part + z
            piece = stacks[part][:, z * 128 : (z + 1) * 128]
            packed = piece.astype(BF16)
            msg[spot, :d] = buf[spot, :d]
            msg[spot, d : 2 * d] = packed[:d]
            both = buf[spot, d : d + 16].astype(F32) + piece[d:]
            msg[spot, 2 * d :] = both.astype(BF16)
            picked = nt(twice, packed)[:8]
            picked = jnp.where((lane == d + 6) & ~hit, LOW, picked)
            picked = jnp.concatenate([picked, jnp.zeros((8, 32), F32)], axis=1)
            rows = buf[spot, d + 16 :].astype(F32)[:8]
            rows = jnp.concatenate([picked, rows], axis=0).astype(BF16)
            for copy in range(shared.shape[0]):
                shared[copy, spot, :16] = got[spot, 3 * d :]
                shared[copy, spot, 16:] = rows


def far_block(got):
    rows = got[:, :, :16, :].astype(F32).reshape(64, 16, 128)
    wide = jnp.concatenate(
        [rows[:, :8].reshape(512, 128), rows[:, 8:].reshape(512, 128)], axis=1
    )
    return wide.T.astype(BF16)


def column_rows():
    return pl.ds(pl.multiple_of(lax.axis_index("seq") // 8 * 64, 64), 64)


def far_forward_kernel(d, factor, got, near, norm, msg, turned):
    block = far_block(got)
    tokens = block.shape[1]
    diag = causal_mask(tokens // 2)
    o, n = forward(block[:d], block[d : 2 * d], block[2 * d : 3 * d], factor, diag)
    norm[...] = jnp.broadcast_to(n, norm.shape)
    stack = jnp.concatenate([o, *split3(n), jnp.zeros((125 - d, tokens), F32)], axis=0)
    turned[...] = stack.T
    mine = turned[column_rows(), :].reshape(8, 8, 128)
    msg[:, : 2 * d + 16] = near[...]
    rows = got[:, :, 16:, :].astype(F32)
    for h in range(msg.shape[0]):
        far = rows[:, h, 8:, :].reshape(64, 128)
        msg[h, 2 * d + 16 : 2 * d + 80] = far.astype(BF16)
    msg[:, 2 * d + 80 :] = jnp.concatenate([mine, jnp.zeros_like(mine)], axis=1).astype(BF16)


def near_stats(d, stats, outs, part):
    g = segment(stats, 0, d, part).astype(F32)
    rest = segment(stats, 2 * d, 16, part).astype(F32)
    o = segment(outs, d, d, part).astype(F32)
    product = jnp.sum(g * o, axis=0, keepdims=True)
    return g, sum3(rest, 0, 0), sum3(rest, 3, 0), product


def owner_backward_kernel(
    heads, d, factor, scale, offsets, got, stats, mine, outs, near_norm, plane_got,
    far_norm, msg, rows_buf, turned,
):
    rows_buf[...] = stats[:, 2 * d + 16 : 2 * d + 80].astype(F32)
    near_offset, far_offset = my_offsets(offsets, heads)
    same = overlap(near_offset, far_offset)
    hit = jnp.max(jnp.where(same, 1.0, 0.0), axis=0, keepdims=True) > 0.5
    tokens = near_norm.shape[1]
    diag = causal_mask(tokens // 2)
    plane = pl.ds(pl.multiple_of(lax.axis_index("seq") // 8 * 8, 8), 8)
    lane = iota((8, 128), 1)
    for part in range(2):
        g, local_norm, local_dot, near_dot = near_stats(d, stats, outs, part)
        far_norms, far_dots = [], []
        for z in range(NEAR):
            rows = mine[4 * part + z, 2 * d + 80 :, :].astype(F32)[:8]
            grads = rows_buf[4 * part + z, plane, :]
            dot = jnp.sum(jnp.where(lane < d, rows * grads, 0.0), axis=1, keepdims=True)
            log = jnp.sum(jnp.where(same, sum3(rows, d, 1), 0.0), axis=0, keepdims=True)
            far_norms.append(jnp.where(hit, log, NEG))
            far_dots.append(jnp.sum(jnp.where(same, dot, 0.0), axis=0, keepdims=True))
        extra = jnp.concatenate(far_norms, axis=1)
        extra_dot = jnp.concatenate(far_dots, axis=1)
        own = near_norm[part : part + 1, :]
        norm = log2_add(log2_add(own, local_norm), extra)
        delta = jnp.exp2(own - norm) * near_dot + jnp.exp2(local_norm - norm) * local_dot
        delta = delta + jnp.exp2(extra - norm) * extra_dot
        qt, kt, vt = [segment(got, i * d, d, part) for i in range(3)]
        grads = backward(qt, kt, vt, g.astype(BF16), norm, delta, factor, scale, diag)
        for slot in range(3):
            packed = grads[slot].astype(BF16)
            for z in range(NEAR):
                msg[4 * part + z, slot * d : (slot + 1) * d] = packed[:, z * 128 : (z + 1) * 128]
    block = far_block(plane_got)
    qt, kt, vt = block[:d], block[d : 2 * d], block[2 * d : 3 * d]
    pieces = [rows_buf[z, 8 * a : 8 * a + 8, :] for a in range(8) for z in range(heads)]
    rows = jnp.concatenate(pieces, axis=0).T
    near = plane_got[:, :, 16:, :].astype(F32)[:, :, :8, :].reshape(tokens, 128).T
    gt = rows[:d].astype(BF16)
    local_norm, other_norm = sum3(rows, d, 0), sum3(near, d + 6, 0)
    own = far_norm[:1, :]
    norm = log2_add(log2_add(own, local_norm), other_norm)
    share = jnp.exp2(own - norm)
    rest = jnp.exp2(local_norm - norm) * sum3(rows, d + 3, 0)
    other = jnp.sum(rows[:d] * near[:d], axis=0, keepdims=True)
    rest = rest + jnp.exp2(other_norm - norm) * other
    dq, dk, dv = backward(qt, kt, vt, gt, own, rest, factor, scale, diag, share)
    stack = jnp.concatenate([dq, dk, dv, jnp.zeros((256 - 3 * d, tokens), F32)], axis=0)
    turned[...] = stack.T
    picked = turned[column_rows(), :]
    msg[:, 3 * d :] = jnp.concatenate(
        [picked[:, :128].reshape(8, 8, 128), picked[:, 128:].reshape(8, 8, 128)], axis=1
    ).astype(BF16)


def local_backward_kernel(
    heads, d, factor, scale, offsets, qkvt, gt, l_out, l_norm, got, attended, grads,
    buf, o_buf, turned, rows_buf, res, sems, load_sems, out_sems,
):
    tokens = gt.shape[1]
    count = tokens // NEAR
    first = [fetch(l_out, o_buf, sems.at[0]), fetch(gt, buf.at[3], sems.at[1])]
    loads = [fetch(qkvt.at[i], buf.at[i], load_sems.at[i]) for i in range(3)]
    lane = iota((1, tokens), 1)
    diag = causal_mask(tokens // 2)
    wait_all(first)
    norms, deltas = [], []
    for h in range(heads):
        rows = slice(h * d, (h + 1) * d)
        near = nn(got[h, d : 2 * d + 16, :], place_matrix(tokens, count, offsets[0, h]))
        near_norm = jnp.where(lane % NEAR == offsets[0, h], sum3(near, d + 6, 0), NEG)
        place = iota((8, tokens), 1) == iota((8, tokens), 0) * 64 + offsets[1, h]
        came = got[h, 2 * d + 80 :, :].astype(F32)[:8]
        spread = jnp.sum(jnp.where(place, sum3(came, d, 1), 0.0), axis=0, keepdims=True)
        far_norm = jnp.where(lane % 64 == offsets[1, h], spread, NEG)
        far_out = tn(came[:, :d].astype(BF16), one_hot(place))
        mine = l_norm[h : h + 1, :]
        both = log2_add(log2_add(mine, near_norm), far_norm)
        mixed = jnp.exp2(mine - both) * o_buf[rows].astype(F32)
        mixed = mixed + jnp.exp2(near_norm - both) * near[:d]
        mixed = (mixed + jnp.exp2(far_norm - both) * far_out).astype(BF16)
        turned[rows, :] = mixed
        delta = buf[3, rows].astype(F32) * mixed.astype(F32)
        norms.append(both)
        deltas.append(jnp.sum(delta, axis=0, keepdims=True))
    rows_buf[...] = turned[...].T
    store = fetch(rows_buf, attended, out_sems.at[0])
    wait_all(loads)
    size = heads // 2 * d
    stores = [store]
    for part in range(2):
        for h in range(part * heads // 2, (part + 1) * heads // 2):
            rows = slice(h * d, (h + 1) * d)
            parts = backward(
                buf[0, rows], buf[1, rows], buf[2, rows], buf[3, rows],
                norms[h], deltas[h], factor, scale, diag,
            )
            for slot in range(3):
                res[slot, rows] = parts[slot].astype(res.dtype)
        half = pl.ds(part * size, size)
        for slot in range(3):
            stores.append(
                fetch(res.at[slot, half], grads.at[slot, half], out_sems.at[1 + 3 * part + slot])
            )
    wait_all(stores)


def final_kernel(heads, d, offsets, grads, got, dq, dk, dv, turned, rows_buf, out_sems):
    tokens = grads.shape[2]
    count = tokens // NEAR
    for h in range(heads):
        rows = slice(h * d, (h + 1) * d)
        total = nn(got[h, : 3 * d], place_matrix(tokens, count, offsets[0, h]))
        place = one_hot(iota((8, tokens), 1) == iota((8, tokens), 0) * 64 + offsets[1, h])
        far = got[h, 3 * d :].astype(F32)
        far = jnp.concatenate([far[:8], far[8:]], axis=1).astype(BF16)
        total = total + tn(far, place)[: 3 * d]
        for slot in range(3):
            mine = total[slot * d : (slot + 1) * d] + grads[slot, rows].astype(F32)
            turned[slot, rows, :] = mine.astype(BF16)
    stores = []
    for slot, ref in enumerate((dq, dk, dv)):
        rows_buf[slot] = turned[slot].T
        stores.append(fetch(rows_buf.at[slot], ref, out_sems.at[slot]))
    wait_all(stores)


def call(kernel, name, operands, outs, scratch=(), limit=63_000_000):
    spaces = {"s": pltpu.SMEM, "v": pltpu.VMEM, "h": pltpu.HBM}
    arrays = [x for x, _ in operands]
    shapes = [x for x, _ in outs]
    return pl.pallas_call(
        kernel,
        name=name,
        out_shape=shapes,
        in_specs=[pl.BlockSpec(memory_space=spaces[where]) for _, where in operands],
        out_specs=[pl.BlockSpec(memory_space=spaces[where]) for _, where in outs],
        scratch_shapes=list(scratch),
        compiler_params=pltpu.CompilerParams(vmem_limit_bytes=limit),
        cost_estimate=pl.CostEstimate(flops=1000, bytes_accessed=1000, transcendentals=0),
    )(*arrays)


def after(x, y):
    return lax.optimization_barrier((x, y))[0]


def on_device(query_rows, key_rows, value_rows, out_weight, cotangent, offsets):
    tokens, width = query_rows.shape
    heads = offsets.shape[1]
    d = width // heads
    scale = 1.0 / math.sqrt(d)
    factor = scale * LOG2E
    seq_size = lax.axis_size("seq")
    count = tokens // NEAR
    groups = seq_size // heads
    columns = [[a * heads + z for z in range(heads)] for a in range(groups)]
    planes = [[a * heads + z for a in range(groups)] for z in range(heads)]
    struct = jax.ShapeDtypeStruct
    dma = pltpu.SemaphoreType.DMA

    def vmem(*shape, dtype=BF16):
        return pltpu.VMEM(shape, dtype)

    def along_column(x):
        return lax.all_to_all(x, "seq", 0, 0, tiled=True, axis_index_groups=columns)

    def over_plane(copies):
        return lax.all_to_all(copies, "seq", 0, 0, tiled=True, axis_index_groups=planes)

    def flipped(x, bit):
        return lax.ppermute(x, "head", [(i, i ^ bit) for i in range(4)])

    c2 = flipped(cotangent, 2)
    c1 = flipped(cotangent, 1)
    qkvt, rows_msg, l_out, l_norm = call(
        functools.partial(local_kernel, heads, factor),
        "local_forward",
        [(offsets, "s"), (query_rows, "h"), (key_rows, "h"), (value_rows, "h")],
        [
            (struct((3, width, tokens), BF16), "h"),
            (struct((heads, 256, count), BF16), "h"),
            (struct((width, tokens), BF16), "h"),
            (struct((heads, tokens), F32), "v"),
        ],
        scratch=[
            vmem(3, tokens, width),
            vmem(3, width, tokens),
            vmem(heads, 256, count),
            vmem(width, tokens),
            dma((3,)),
            dma((6,)),
        ],
    )
    rows_got = along_column(rows_msg)
    c2 = after(c2, l_norm)
    c3 = flipped(c2, 1)
    gt, stats_msg = call(
        functools.partial(stats_kernel, heads, d),
        "stats",
        [(offsets, "s"), (out_weight, "h")]
        + [(x, "h") for x in (cotangent, c1, c2, c3)]
        + [(l_out, "h"), (l_norm, "v")],
        [
            (struct((width, tokens), BF16), "h"),
            (struct((heads, 112, 128), BF16), "v"),
        ],
        scratch=[
            vmem(4, width, width),
            vmem(4, tokens, width),
            vmem(width, tokens),
            vmem(width, tokens),
            dma((9,)),
            dma((1,)),
        ],
    )
    rows_got = after(rows_got, stats_msg)
    near_out, near_norm, shared = call(
        functools.partial(near_forward_kernel, heads, d, factor),
        "near_forward",
        [(offsets, "s"), (rows_got, "v"), (stats_msg, "h")],
        [
            (struct((heads, 176, count), BF16), "v"),
            (struct((2, tokens), F32), "v"),
            (struct((groups, heads, 32, 128), BF16), "v"),
        ],
        scratch=[vmem(heads, 112, 128), dma((1,))],
        limit=16_000_000,
    )
    far_got = over_plane(shared)
    far_norm, swap_msg = call(
        functools.partial(far_forward_kernel, d, factor),
        "far_forward",
        [(far_got, "v"), (near_out, "v")],
        [
            (struct((8, tokens), F32), "v"),
            (struct((heads, 256, 128), BF16), "v"),
        ],
        scratch=[vmem(tokens, 128, dtype=F32)],
        limit=16_000_000,
    )
    swap_got = along_column(swap_msg)
    (grad_msg,) = call(
        functools.partial(owner_backward_kernel, heads, d, factor, scale),
        "owner_backward",
        [(offsets, "s"), (rows_got, "v"), (swap_got, "v"), (swap_msg, "v"), (near_out, "v")]
        + [(near_norm, "v"), (far_got, "v"), (far_norm, "v")],
        [(struct((heads, 256, 128), BF16), "v")],
        scratch=[
            vmem(heads, 64, 128, dtype=F32),
            vmem(tokens, 256, dtype=F32),
        ],
        limit=16_000_000,
    )
    owner_grads = along_column(grad_msg)
    swap_got = after(swap_got, grad_msg)
    attended, grads = call(
        functools.partial(local_backward_kernel, heads, d, factor, scale),
        "local_backward",
        [(offsets, "s"), (qkvt, "h"), (gt, "h"), (l_out, "h"), (l_norm, "v"), (swap_got, "v")],
        [
            (struct((tokens, width), BF16), "h"),
            (struct((3, width, tokens), BF16), "h"),
        ],
        scratch=[
            vmem(4, width, tokens),
            vmem(width, tokens),
            vmem(width, tokens),
            vmem(tokens, width),
            vmem(3, width, tokens),
            dma((2,)),
            dma((3,)),
            dma((7,)),
        ],
    )
    grad_query, grad_key, grad_value = call(
        functools.partial(final_kernel, heads, d),
        "final",
        [(offsets, "s"), (grads, "v"), (owner_grads, "v")],
        [(struct((tokens, width), BF16), "h")] * 3,
        scratch=[
            vmem(3, width, tokens),
            vmem(3, tokens, width),
            dma((3,)),
        ],
        limit=16_000_000,
    )
    return (attended, grad_query, grad_key, grad_value)


def solution(mesh):
    return jax.shard_map(
        on_device,
        mesh=mesh,
        in_specs=(
            P("seq", "head"),
            P("seq", "head"),
            P("seq", "head"),
            P("head", None),
            P("seq", "head"),
            P(None, "head"),
        ),
        out_specs=(P("seq", "head"), P("seq", "head"), P("seq", "head"), P("seq", "head")),
        check_vma=False,
    )
```

```python
import functools
import math

import jax
import jax.numpy as jnp
from jax import lax
from jax.experimental import pallas as pl
from jax.experimental.pallas import tpu as pltpu
from jax.sharding import PartitionSpec as P

NEAR = 4
F32 = jnp.float32
BF16 = jnp.bfloat16
LOG2E = math.log2(math.e)
NEG = float("-inf")
LOW = -1e30


def nn(a, b):
    return lax.dot_general(a, b, (((1,), (0,)), ((), ())), preferred_element_type=F32)


def nt(a, b):
    return lax.dot_general(a, b, (((1,), (1,)), ((), ())), preferred_element_type=F32)


def tn(a, b):
    return lax.dot_general(a, b, (((0,), (0,)), ((), ())), preferred_element_type=F32)


def iota(shape, dim):
    return lax.broadcasted_iota(jnp.int32, shape, dim)


def one_hot(mask):
    return jnp.where(mask, 1.0, 0.0).astype(BF16)


def pick_matrix(tokens, count, offset):
    rate = tokens // count
    return one_hot(iota((tokens, count), 0) == iota((tokens, count), 1) * rate + offset)


def place_matrix(tokens, count, offset, rows=None):
    rate = tokens // count
    rows = rows or count
    return one_hot(iota((rows, tokens), 1) == iota((rows, tokens), 0) * rate + offset)


def split3(x):
    high = x.astype(BF16).astype(F32)
    rest = x - high
    middle = rest.astype(BF16).astype(F32)
    return high, middle, rest - middle


def log2_add(a, b):
    top = jnp.maximum(a, b)
    return top + jnp.log(jnp.exp2(a - top) + jnp.exp2(b - top)) * LOG2E


def causal_mask(size):
    return iota((size, size), 0) <= iota((size, size), 1)


def halves(tokens):
    half = tokens // 2
    return half, ((0, slice(0, half)), (1, slice(half, tokens)))


def forward(qt, kt, vt, factor, diag):
    tokens = qt.shape[1]
    half, blocks = halves(tokens)
    outs, norms = [], []
    for index, cols in blocks:
        keys = (index + 1) * half
        scores = tn(kt[:, :keys], qt[:, cols])
        last = jnp.where(diag, scores[keys - half :], NEG)
        parts = [last] if index == 0 else [scores[:half], last]
        top = functools.reduce(
            jnp.maximum, [jnp.max(part, axis=0, keepdims=True) for part in parts]
        )
        top = top * factor
        probs = [jnp.exp2(part * factor - top) for part in parts]
        total = sum(jnp.sum(part, axis=0, keepdims=True) for part in probs)
        packed = [part.astype(BF16) for part in probs]
        packed = packed[0] if index == 0 else jnp.concatenate(packed, axis=0)
        outs.append(nn(vt[:, :keys], packed) / total)
        norms.append(top + jnp.log(total) * LOG2E)
    return jnp.concatenate(outs, axis=1), jnp.concatenate(norms, axis=1)


def backward(qt, kt, vt, gt, norm, delta, factor, scale, diag, share=None):
    tokens = qt.shape[1]
    half, blocks = halves(tokens)
    dq = []
    for index, cols in blocks:
        keys = (index + 1) * half
        scores = tn(kt[:, :keys], qt[:, cols]) * factor - norm[:, cols]
        last = jnp.where(diag, jnp.exp2(scores[keys - half :]), 0.0)
        if index == 0:
            probs = last
        else:
            probs = jnp.concatenate([jnp.exp2(scores[:half]), last], axis=0)
        dprobs = tn(vt[:, :keys], gt[:, cols])
        total = delta[:, cols]
        if share is not None:
            mine = jnp.sum(probs * dprobs, axis=0, keepdims=True)
            total = total + share[:, cols] * mine
            probs = probs * share[:, cols]
        dscores = (probs * (dprobs - total)).astype(BF16)
        dq.append(nn(kt[:, :keys], dscores) * scale)
        dk_part = nt(qt[:, cols], dscores) * scale
        dv_part = nt(gt[:, cols], probs.astype(BF16))
        if index == 0:
            dk, dv = dk_part, dv_part
        else:
            dk = jnp.concatenate([dk + dk_part[:, :half], dk_part[:, half:]], axis=1)
            dv = jnp.concatenate([dv + dv_part[:, :half], dv_part[:, half:]], axis=1)
    return jnp.concatenate(dq, axis=1), dk, dv


def fetch(src, dst, sem):
    copy = pltpu.make_async_copy(src, dst, sem)
    copy.start()
    return copy


def both_halves(pairs, sems, size):
    return [
        [
            fetch(src.at[pl.ds(i * size, size)], dst.at[pl.ds(i * size, size)], sems.at[i, j])
            for j, (src, dst) in enumerate(pairs)
        ]
        for i in range(2)
    ]


def wait_all(copies):
    for copy in copies:
        copy.wait()


def my_offsets(offsets, heads):
    mine = lax.axis_index("seq") % heads
    return offsets[0, mine], offsets[1, mine]


def sum3(x, first, axis):
    if axis == 0:
        return x[first : first + 1] + x[first + 1 : first + 2] + x[first + 2 : first + 3]
    return x[:, first : first + 1] + x[:, first + 1 : first + 2] + x[:, first + 2 : first + 3]


def local_kernel(
    heads, factor, offsets, q, k, v, qkvt, msg, out, norm, raw, turned, sent, res, sems, out_sems
):
    tokens, width = q.shape
    d = width // heads
    loads = [fetch(ref, raw.at[i], sems.at[i]) for i, ref in enumerate((q, k, v))]
    stores = []
    for slot in range(3):
        loads[slot].wait()
        turned[slot] = raw[slot].T
        stores.append(fetch(turned.at[slot], qkvt.at[slot], out_sems.at[slot]))
    diag = causal_mask(tokens // 2)
    for h in range(heads):
        rows = slice(h * d, (h + 1) * d)
        block = jnp.concatenate([turned[0, rows], turned[1, rows], turned[2, rows]], axis=0)
        near = nn(block, pick_matrix(tokens, tokens // NEAR, offsets[0, h]))
        sent[h, : 3 * d] = near.astype(BF16)
        picked = nt(place_matrix(tokens, 8, offsets[1, h], 16), block)[:8]
        tail = jnp.concatenate([picked[:, 128:], jnp.zeros((8, 256 - 3 * d), F32)], axis=1)
        sent[h, 3 * d :] = jnp.concatenate([picked[:, :128], tail], axis=0).astype(BF16)
    stores.append(fetch(sent, msg, out_sems.at[3]))
    size = heads // 2 * d
    for part in range(2):
        for h in range(part * heads // 2, (part + 1) * heads // 2):
            rows = slice(h * d, (h + 1) * d)
            o, n = forward(turned[0, rows], turned[1, rows], turned[2, rows], factor, diag)
            res[rows] = o.astype(BF16)
            norm[h : h + 1, :] = n
        half = pl.ds(part * size, size)
        stores.append(fetch(res.at[half], out.at[half], out_sems.at[4 + part]))
    wait_all(stores)


def stats_kernel(
    heads, d, offsets, w, c0, c1, c2, c3, l_out, l_norm, gt, msg,
    w_buf, c_buf, l_buf, g_buf, sems, out_sems,
):
    tokens, width = c0.shape
    count = tokens // NEAR
    head = lax.axis_index("head")
    loads = []
    for flip, ref in enumerate((c0, c1, c2, c3)):
        first = pl.multiple_of(jnp.bitwise_xor(head, flip) * width, 128)
        loads.append(fetch(w.at[:, pl.ds(first, width)], w_buf.at[flip], sems.at[flip]))
        loads.append(fetch(ref, c_buf.at[flip], sems.at[4 + flip]))
    loads.append(fetch(l_out, l_buf, sems.at[8]))
    wait_all(loads[:4])
    grads = nt(w_buf[0], c_buf[0]) + nt(w_buf[1], c_buf[1])
    wait_all(loads[4:])
    grads = grads + nt(w_buf[2], c_buf[2]) + nt(w_buf[3], c_buf[3])
    grads = grads.astype(BF16)
    g_buf[...] = grads
    store = fetch(g_buf, gt, out_sems.at[0])
    for h in range(heads):
        rows = slice(h * d, (h + 1) * d)
        g = grads[rows].astype(F32)
        product = jnp.sum(g * l_buf[rows].astype(F32), axis=0, keepdims=True)
        stack = jnp.concatenate(
            [
                g,
                *split3(l_norm[h : h + 1, :]),
                *split3(product),
                jnp.zeros((122 - d, tokens), F32),
            ],
            axis=0,
        ).astype(BF16)
        near = nn(stack[:96], pick_matrix(tokens, count, offsets[0, h]))
        far = nt(place_matrix(tokens, 8, offsets[1, h], 16), stack)
        msg[h] = jnp.concatenate([near, far], axis=0).astype(BF16)
    store.wait()


def segment(got, first, size, part):
    pieces = [got[4 * part + z, first : first + size, :] for z in range(NEAR)]
    return jnp.concatenate(pieces, axis=1)


def overlap(near_offset, far_offset):
    shift = far_offset - near_offset
    spot = iota((8, 128), 0) * 16 + lax.shift_right_arithmetic(shift, 2)
    return (iota((8, 128), 1) == spot) & (lax.bitwise_and(shift, 3) == 0)


def near_forward_kernel(heads, d, factor, offsets, got, stats, msg, norm, shared, buf, sems):
    tokens = NEAR * got.shape[2]
    load = fetch(stats, buf, sems.at[0])
    diag = causal_mask(tokens // 2)
    same = overlap(*my_offsets(offsets, heads))
    hit = jnp.max(jnp.where(same, 1.0, 0.0), axis=1, keepdims=True) > 0.5
    twice = one_hot(jnp.concatenate([same, same], axis=0))
    lane = iota((8, 96), 1)
    stacks = []
    for part in range(2):
        qt, kt, vt = [segment(got, i * d, d, part) for i in range(3)]
        o, n = forward(qt, kt, vt, factor, diag)
        norm[part : part + 1, :] = n
        gap = jnp.zeros((6, tokens), F32)
        rest = jnp.zeros((87 - d, tokens), F32)
        stacks.append(jnp.concatenate([o, gap, *split3(n), rest], axis=0))
    load.wait()
    for part in range(2):
        for z in range(NEAR):
            spot = 4 * part + z
            piece = stacks[part][:, z * 128 : (z + 1) * 128]
            packed = piece.astype(BF16)
            msg[spot, :d] = buf[spot, :d]
            msg[spot, d : 2 * d] = packed[:d]
            both = buf[spot, d : d + 16].astype(F32) + piece[d:]
            msg[spot, 2 * d :] = both.astype(BF16)
            picked = nt(twice, packed)[:8]
            picked = jnp.where((lane == d + 6) & ~hit, LOW, picked)
            picked = jnp.concatenate([picked, jnp.zeros((8, 32), F32)], axis=1)
            rows = buf[spot, d + 16 :].astype(F32)[:8]
            rows = jnp.concatenate([picked, rows], axis=0).astype(BF16)
            for copy in range(shared.shape[0]):
                shared[copy, spot, :16] = got[spot, 3 * d :]
                shared[copy, spot, 16:] = rows


def far_block(got):
    rows = got[:, :, :16, :].astype(F32).reshape(64, 16, 128)
    wide = jnp.concatenate(
        [rows[:, :8].reshape(512, 128), rows[:, 8:].reshape(512, 128)], axis=1
    )
    return wide.T.astype(BF16)


def column_rows():
    return pl.ds(pl.multiple_of(lax.axis_index("seq") // 8 * 64, 64), 64)


def far_forward_kernel(d, factor, got, near, norm, msg, own, turned):
    block = far_block(got)
    tokens = block.shape[1]
    diag = causal_mask(tokens // 2)
    o, n = forward(block[:d], block[d : 2 * d], block[2 * d : 3 * d], factor, diag)
    norm[...] = jnp.broadcast_to(n, norm.shape)
    stack = jnp.concatenate([o, *split3(n), jnp.zeros((125 - d, tokens), F32)], axis=0)
    turned[...] = stack.T
    mine = turned[column_rows(), :].reshape(8, 8, 128)
    msg[:, : 2 * d + 16] = near[...]
    own[...] = mine
    rows = got[:, :, 16:, :].astype(F32)
    used = d + 6
    for h in range(msg.shape[0]):
        far = rows[:, h, 8:, :].reshape(64, 128)
        first = jnp.concatenate([far[:8, :used], mine[h, :, : 128 - used]], axis=1)
        tail = mine[h, :, 128 - used : 2 * (128 - used)]
        second = jnp.concatenate([far[8:16, :used], tail], axis=1)
        far = jnp.concatenate([first, second, far[16:]], axis=0)
        msg[h, 2 * d + 16 :] = far.astype(BF16)


def near_stats(d, stats, outs, part):
    g = segment(stats, 0, d, part).astype(F32)
    rest = segment(stats, 2 * d, 16, part).astype(F32)
    o = segment(outs, d, d, part).astype(F32)
    product = jnp.sum(g * o, axis=0, keepdims=True)
    return g, sum3(rest, 0, 0), sum3(rest, 3, 0), product


def owner_backward_kernel(
    heads, d, factor, scale, offsets, got, stats, mine, outs, near_norm, plane_got,
    far_norm, msg, rows_buf, turned,
):
    rows_buf[...] = stats[:, 2 * d + 16 : 2 * d + 80].astype(F32)
    near_offset, far_offset = my_offsets(offsets, heads)
    same = overlap(near_offset, far_offset)
    hit = jnp.max(jnp.where(same, 1.0, 0.0), axis=0, keepdims=True) > 0.5
    tokens = near_norm.shape[1]
    diag = causal_mask(tokens // 2)
    plane = pl.ds(pl.multiple_of(lax.axis_index("seq") // 8 * 8, 8), 8)
    lane = iota((8, 128), 1)
    for part in range(2):
        g, local_norm, local_dot, near_dot = near_stats(d, stats, outs, part)
        far_norms, far_dots = [], []
        for z in range(NEAR):
            rows = mine[4 * part + z]
            grads = rows_buf[4 * part + z, plane, :]
            dot = jnp.sum(jnp.where(lane < d, rows * grads, 0.0), axis=1, keepdims=True)
            log = jnp.sum(jnp.where(same, sum3(rows, d, 1), 0.0), axis=0, keepdims=True)
            far_norms.append(jnp.where(hit, log, NEG))
            far_dots.append(jnp.sum(jnp.where(same, dot, 0.0), axis=0, keepdims=True))
        extra = jnp.concatenate(far_norms, axis=1)
        extra_dot = jnp.concatenate(far_dots, axis=1)
        own = near_norm[part : part + 1, :]
        norm = log2_add(log2_add(own, local_norm), extra)
        delta = jnp.exp2(own - norm) * near_dot + jnp.exp2(local_norm - norm) * local_dot
        delta = delta + jnp.exp2(extra - norm) * extra_dot
        qt, kt, vt = [segment(got, i * d, d, part) for i in range(3)]
        grads = backward(qt, kt, vt, g.astype(BF16), norm, delta, factor, scale, diag)
        for slot in range(3):
            packed = grads[slot].astype(BF16)
            for z in range(NEAR):
                msg[4 * part + z, slot * d : (slot + 1) * d] = packed[:, z * 128 : (z + 1) * 128]
    block = far_block(plane_got)
    qt, kt, vt = block[:d], block[d : 2 * d], block[2 * d : 3 * d]
    pieces = [rows_buf[z, 8 * a : 8 * a + 8, :] for a in range(8) for z in range(heads)]
    rows = jnp.concatenate(pieces, axis=0).T
    near = plane_got[:, :, 16:, :].astype(F32)[:, :, :8, :].reshape(tokens, 128).T
    gt = rows[:d].astype(BF16)
    local_norm, other_norm = sum3(rows, d, 0), sum3(near, d + 6, 0)
    own = far_norm[:1, :]
    norm = log2_add(log2_add(own, local_norm), other_norm)
    share = jnp.exp2(own - norm)
    rest = jnp.exp2(local_norm - norm) * sum3(rows, d + 3, 0)
    other = jnp.sum(rows[:d] * near[:d], axis=0, keepdims=True)
    rest = rest + jnp.exp2(other_norm - norm) * other
    dq, dk, dv = backward(qt, kt, vt, gt, own, rest, factor, scale, diag, share)
    stack = jnp.concatenate([dq, dk, dv, jnp.zeros((256 - 3 * d, tokens), F32)], axis=0)
    turned[...] = stack.T
    picked = turned[column_rows(), :]
    msg[:, 3 * d :] = jnp.concatenate(
        [picked[:, :128].reshape(8, 8, 128), picked[:, 128:].reshape(8, 8, 128)], axis=1
    ).astype(BF16)


def local_backward_kernel(
    heads, d, factor, scale, offsets, qkvt, gt, l_out, l_norm, got, attended, grads,
    buf, o_buf, turned, rows_buf, res, sems, load_sems, out_sems,
):
    tokens = gt.shape[1]
    count = tokens // NEAR
    first = [fetch(l_out, o_buf, sems.at[0]), fetch(gt, buf.at[3], sems.at[1])]
    loads = [fetch(qkvt.at[i], buf.at[i], load_sems.at[i]) for i in range(3)]
    lane = iota((1, tokens), 1)
    diag = causal_mask(tokens // 2)
    wait_all(first)
    norms, deltas = [], []
    for h in range(heads):
        rows = slice(h * d, (h + 1) * d)
        near = nn(got[h, d : 2 * d + 16, :], place_matrix(tokens, count, offsets[0, h]))
        near_norm = jnp.where(lane % NEAR == offsets[0, h], sum3(near, d + 6, 0), NEG)
        place = iota((8, tokens), 1) == iota((8, tokens), 0) * 64 + offsets[1, h]
        came = got[h, 2 * d + 16 : 2 * d + 32, :].astype(F32)
        came = jnp.concatenate([came[:8, d + 6 :], came[8:, d + 6 :]], axis=1)
        spread = jnp.sum(jnp.where(place, sum3(came, d, 1), 0.0), axis=0, keepdims=True)
        far_norm = jnp.where(lane % 64 == offsets[1, h], spread, NEG)
        far_out = tn(came[:, :d].astype(BF16), one_hot(place))
        mine = l_norm[h : h + 1, :]
        both = log2_add(log2_add(mine, near_norm), far_norm)
        mixed = jnp.exp2(mine - both) * o_buf[rows].astype(F32)
        mixed = mixed + jnp.exp2(near_norm - both) * near[:d]
        mixed = (mixed + jnp.exp2(far_norm - both) * far_out).astype(BF16)
        turned[rows, :] = mixed
        delta = buf[3, rows].astype(F32) * mixed.astype(F32)
        norms.append(both)
        deltas.append(jnp.sum(delta, axis=0, keepdims=True))
    rows_buf[...] = turned[...].T
    store = fetch(rows_buf, attended, out_sems.at[0])
    wait_all(loads)
    size = heads // 2 * d
    stores = [store]
    for part in range(2):
        for h in range(part * heads // 2, (part + 1) * heads // 2):
            rows = slice(h * d, (h + 1) * d)
            parts = backward(
                buf[0, rows], buf[1, rows], buf[2, rows], buf[3, rows],
                norms[h], deltas[h], factor, scale, diag,
            )
            for slot in range(3):
                res[slot, rows] = parts[slot].astype(res.dtype)
        half = pl.ds(part * size, size)
        for slot in range(3):
            stores.append(
                fetch(res.at[slot, half], grads.at[slot, half], out_sems.at[1 + 3 * part + slot])
            )
    wait_all(stores)


def final_kernel(heads, d, offsets, grads, got, dq, dk, dv, turned, rows_buf, out_sems):
    tokens = grads.shape[2]
    count = tokens // NEAR
    for h in range(heads):
        rows = slice(h * d, (h + 1) * d)
        total = nn(got[h, : 3 * d], place_matrix(tokens, count, offsets[0, h]))
        place = one_hot(iota((8, tokens), 1) == iota((8, tokens), 0) * 64 + offsets[1, h])
        far = got[h, 3 * d :].astype(F32)
        far = jnp.concatenate([far[:8], far[8:]], axis=1).astype(BF16)
        total = total + tn(far, place)[: 3 * d]
        for slot in range(3):
            mine = total[slot * d : (slot + 1) * d] + grads[slot, rows].astype(F32)
            turned[slot, rows, :] = mine.astype(BF16)
    stores = []
    for slot, ref in enumerate((dq, dk, dv)):
        rows_buf[slot] = turned[slot].T
        stores.append(fetch(rows_buf.at[slot], ref, out_sems.at[slot]))
    wait_all(stores)


def call(kernel, name, operands, outs, scratch=(), limit=63_000_000):
    spaces = {"s": pltpu.SMEM, "v": pltpu.VMEM, "h": pltpu.HBM}
    arrays = [x for x, _ in operands]
    shapes = [x for x, _ in outs]
    return pl.pallas_call(
        kernel,
        name=name,
        out_shape=shapes,
        in_specs=[pl.BlockSpec(memory_space=spaces[where]) for _, where in operands],
        out_specs=[pl.BlockSpec(memory_space=spaces[where]) for _, where in outs],
        scratch_shapes=list(scratch),
        compiler_params=pltpu.CompilerParams(vmem_limit_bytes=limit),
        cost_estimate=pl.CostEstimate(flops=1000, bytes_accessed=1000, transcendentals=0),
    )(*arrays)


def after(x, y):
    return lax.optimization_barrier((x, y))[0]


def on_device(query_rows, key_rows, value_rows, out_weight, cotangent, offsets):
    tokens, width = query_rows.shape
    heads = offsets.shape[1]
    d = width // heads
    scale = 1.0 / math.sqrt(d)
    factor = scale * LOG2E
    seq_size = lax.axis_size("seq")
    count = tokens // NEAR
    groups = seq_size // heads
    columns = [[a * heads + z for z in range(heads)] for a in range(groups)]
    planes = [[a * heads + z for a in range(groups)] for z in range(heads)]
    struct = jax.ShapeDtypeStruct
    dma = pltpu.SemaphoreType.DMA

    def vmem(*shape, dtype=BF16):
        return pltpu.VMEM(shape, dtype)

    def along_column(x):
        return lax.all_to_all(x, "seq", 0, 0, tiled=True, axis_index_groups=columns)

    def over_plane(copies):
        return lax.all_to_all(copies, "seq", 0, 0, tiled=True, axis_index_groups=planes)

    def flipped(x, bit):
        return lax.ppermute(x, "head", [(i, i ^ bit) for i in range(4)])

    c2 = flipped(cotangent, 2)
    c1 = flipped(cotangent, 1)
    qkvt, rows_msg, l_out, l_norm = call(
        functools.partial(local_kernel, heads, factor),
        "local_forward",
        [(offsets, "s"), (query_rows, "h"), (key_rows, "h"), (value_rows, "h")],
        [
            (struct((3, width, tokens), BF16), "h"),
            (struct((heads, 256, count), BF16), "h"),
            (struct((width, tokens), BF16), "h"),
            (struct((heads, tokens), F32), "v"),
        ],
        scratch=[
            vmem(3, tokens, width),
            vmem(3, width, tokens),
            vmem(heads, 256, count),
            vmem(width, tokens),
            dma((3,)),
            dma((6,)),
        ],
    )
    rows_got = along_column(rows_msg)
    c2 = after(c2, l_norm)
    c3 = flipped(c2, 1)
    gt, stats_msg = call(
        functools.partial(stats_kernel, heads, d),
        "stats",
        [(offsets, "s"), (out_weight, "h")]
        + [(x, "h") for x in (cotangent, c1, c2, c3)]
        + [(l_out, "h"), (l_norm, "v")],
        [
            (struct((width, tokens), BF16), "h"),
            (struct((heads, 112, 128), BF16), "v"),
        ],
        scratch=[
            vmem(4, width, width),
            vmem(4, tokens, width),
            vmem(width, tokens),
            vmem(width, tokens),
            dma((9,)),
            dma((1,)),
        ],
    )
    rows_got = after(rows_got, stats_msg)
    near_out, near_norm, shared = call(
        functools.partial(near_forward_kernel, heads, d, factor),
        "near_forward",
        [(offsets, "s"), (rows_got, "v"), (stats_msg, "h")],
        [
            (struct((heads, 176, count), BF16), "v"),
            (struct((2, tokens), F32), "v"),
            (struct((groups, heads, 32, 128), BF16), "v"),
        ],
        scratch=[vmem(heads, 112, 128), dma((1,))],
        limit=16_000_000,
    )
    far_got = over_plane(shared)
    far_norm, swap_msg, own_far = call(
        functools.partial(far_forward_kernel, d, factor),
        "far_forward",
        [(far_got, "v"), (near_out, "v")],
        [
            (struct((8, tokens), F32), "v"),
            (struct((heads, 240, 128), BF16), "v"),
            (struct((heads, 8, 128), F32), "v"),
        ],
        scratch=[vmem(tokens, 128, dtype=F32)],
        limit=16_000_000,
    )
    swap_got = along_column(swap_msg)
    (grad_msg,) = call(
        functools.partial(owner_backward_kernel, heads, d, factor, scale),
        "owner_backward",
        [(offsets, "s"), (rows_got, "v"), (swap_got, "v"), (own_far, "v"), (near_out, "v")]
        + [(near_norm, "v"), (far_got, "v"), (far_norm, "v")],
        [(struct((heads, 256, 128), BF16), "v")],
        scratch=[
            vmem(heads, 64, 128, dtype=F32),
            vmem(tokens, 256, dtype=F32),
        ],
        limit=16_000_000,
    )
    owner_grads = along_column(grad_msg)
    swap_got = after(swap_got, grad_msg)
    attended, grads = call(
        functools.partial(local_backward_kernel, heads, d, factor, scale),
        "local_backward",
        [(offsets, "s"), (qkvt, "h"), (gt, "h"), (l_out, "h"), (l_norm, "v"), (swap_got, "v")],
        [
            (struct((tokens, width), BF16), "h"),
            (struct((3, width, tokens), BF16), "h"),
        ],
        scratch=[
            vmem(4, width, tokens),
            vmem(width, tokens),
            vmem(width, tokens),
            vmem(tokens, width),
            vmem(3, width, tokens),
            dma((2,)),
            dma((3,)),
            dma((7,)),
        ],
    )
    grad_query, grad_key, grad_value = call(
        functools.partial(final_kernel, heads, d),
        "final",
        [(offsets, "s"), (grads, "v"), (owner_grads, "v")],
        [(struct((tokens, width), BF16), "h")] * 3,
        scratch=[
            vmem(3, width, tokens),
            vmem(3, tokens, width),
            dma((3,)),
        ],
        limit=16_000_000,
    )
    return (attended, grad_query, grad_key, grad_value)


def solution(mesh):
    return jax.shard_map(
        on_device,
        mesh=mesh,
        in_specs=(
            P("seq", "head"),
            P("seq", "head"),
            P("seq", "head"),
            P("head", None),
            P("seq", "head"),
            P(None, "head"),
        ),
        out_specs=(P("seq", "head"), P("seq", "head"), P("seq", "head"), P("seq", "head")),
        check_vma=False,
    )
```

```python
import functools
import math

import jax
import jax.numpy as jnp
from jax import lax
from jax.experimental import pallas as pl
from jax.experimental.pallas import tpu as pltpu
from jax.sharding import PartitionSpec as P

NEAR = 4
F32 = jnp.float32
BF16 = jnp.bfloat16
LOG2E = math.log2(math.e)
NEG = float("-inf")
LOW = -1e30


def nn(a, b):
    return lax.dot_general(a, b, (((1,), (0,)), ((), ())), preferred_element_type=F32)


def nt(a, b):
    return lax.dot_general(a, b, (((1,), (1,)), ((), ())), preferred_element_type=F32)


def tn(a, b):
    return lax.dot_general(a, b, (((0,), (0,)), ((), ())), preferred_element_type=F32)


def iota(shape, dim):
    return lax.broadcasted_iota(jnp.int32, shape, dim)


def one_hot(mask):
    return jnp.where(mask, 1.0, 0.0).astype(BF16)


def pick_matrix(tokens, count, offset):
    rate = tokens // count
    return one_hot(iota((tokens, count), 0) == iota((tokens, count), 1) * rate + offset)


def place_matrix(tokens, count, offset, rows=None):
    rate = tokens // count
    rows = rows or count
    return one_hot(iota((rows, tokens), 1) == iota((rows, tokens), 0) * rate + offset)


def split3(x):
    high = x.astype(BF16).astype(F32)
    rest = x - high
    middle = rest.astype(BF16).astype(F32)
    return high, middle, rest - middle


def log2_add(a, b):
    top = jnp.maximum(a, b)
    return top + jnp.log(jnp.exp2(a - top) + jnp.exp2(b - top)) * LOG2E


def causal_mask(size):
    return iota((size, size), 0) <= iota((size, size), 1)


def halves(tokens):
    half = tokens // 2
    return half, ((0, slice(0, half)), (1, slice(half, tokens)))


def forward(qt, kt, vt, factor, diag):
    tokens = qt.shape[1]
    half, blocks = halves(tokens)
    outs, norms = [], []
    for index, cols in blocks:
        keys = (index + 1) * half
        scores = tn(kt[:, :keys], qt[:, cols])
        last = jnp.where(diag, scores[keys - half :], NEG)
        parts = [last] if index == 0 else [scores[:half], last]
        top = functools.reduce(
            jnp.maximum, [jnp.max(part, axis=0, keepdims=True) for part in parts]
        )
        top = top * factor
        probs = [jnp.exp2(part * factor - top) for part in parts]
        total = sum(jnp.sum(part, axis=0, keepdims=True) for part in probs)
        packed = [part.astype(BF16) for part in probs]
        packed = packed[0] if index == 0 else jnp.concatenate(packed, axis=0)
        outs.append(nn(vt[:, :keys], packed) / total)
        norms.append(top + jnp.log(total) * LOG2E)
    return jnp.concatenate(outs, axis=1), jnp.concatenate(norms, axis=1)


def backward(qt, kt, vt, gt, norm, delta, factor, scale, diag, share=None):
    tokens = qt.shape[1]
    half, blocks = halves(tokens)
    dq = []
    for index, cols in blocks:
        keys = (index + 1) * half
        scores = tn(kt[:, :keys], qt[:, cols]) * factor - norm[:, cols]
        last = jnp.where(diag, jnp.exp2(scores[keys - half :]), 0.0)
        if index == 0:
            probs = last
        else:
            probs = jnp.concatenate([jnp.exp2(scores[:half]), last], axis=0)
        dprobs = tn(vt[:, :keys], gt[:, cols])
        total = delta[:, cols]
        if share is not None:
            mine = jnp.sum(probs * dprobs, axis=0, keepdims=True)
            total = total + share[:, cols] * mine
            probs = probs * share[:, cols]
        dscores = (probs * (dprobs - total)).astype(BF16)
        dq.append(nn(kt[:, :keys], dscores) * scale)
        dk_part = nt(qt[:, cols], dscores) * scale
        dv_part = nt(gt[:, cols], probs.astype(BF16))
        if index == 0:
            dk, dv = dk_part, dv_part
        else:
            dk = jnp.concatenate([dk + dk_part[:, :half], dk_part[:, half:]], axis=1)
            dv = jnp.concatenate([dv + dv_part[:, :half], dv_part[:, half:]], axis=1)
    return jnp.concatenate(dq, axis=1), dk, dv


def fetch(src, dst, sem):
    copy = pltpu.make_async_copy(src, dst, sem)
    copy.start()
    return copy


def both_halves(pairs, sems, size):
    return [
        [
            fetch(src.at[pl.ds(i * size, size)], dst.at[pl.ds(i * size, size)], sems.at[i, j])
            for j, (src, dst) in enumerate(pairs)
        ]
        for i in range(2)
    ]


def wait_all(copies):
    for copy in copies:
        copy.wait()


def my_offsets(offsets, heads):
    mine = lax.axis_index("seq") % heads
    return offsets[0, mine], offsets[1, mine]


def sum3(x, first, axis):
    if axis == 0:
        return x[first : first + 1] + x[first + 1 : first + 2] + x[first + 2 : first + 3]
    return x[:, first : first + 1] + x[:, first + 1 : first + 2] + x[:, first + 2 : first + 3]


def local_kernel(
    heads, factor, offsets, q, k, v, qkvt, msg, out, norm, raw, turned, sent, res, sems, out_sems
):
    tokens, width = q.shape
    d = width // heads
    loads = [fetch(ref, raw.at[i], sems.at[i]) for i, ref in enumerate((q, k, v))]
    stores = []
    for slot in range(3):
        loads[slot].wait()
        turned[slot] = raw[slot].T
        stores.append(fetch(turned.at[slot], qkvt.at[slot], out_sems.at[slot]))
    diag = causal_mask(tokens // 2)
    for h in range(heads):
        rows = slice(h * d, (h + 1) * d)
        block = jnp.concatenate([turned[0, rows], turned[1, rows], turned[2, rows]], axis=0)
        near = nn(block, pick_matrix(tokens, tokens // NEAR, offsets[0, h]))
        sent[h, : 3 * d] = near.astype(BF16)
        picked = nt(place_matrix(tokens, 8, offsets[1, h], 16), block)[:8]
        tail = jnp.concatenate([picked[:, 128:], jnp.zeros((8, 256 - 3 * d), F32)], axis=1)
        sent[h, 3 * d :] = jnp.concatenate([picked[:, :128], tail], axis=0).astype(BF16)
    stores.append(fetch(sent, msg, out_sems.at[3]))
    size = heads // 2 * d
    for part in range(2):
        for h in range(part * heads // 2, (part + 1) * heads // 2):
            rows = slice(h * d, (h + 1) * d)
            o, n = forward(turned[0, rows], turned[1, rows], turned[2, rows], factor, diag)
            res[rows] = o.astype(BF16)
            norm[h : h + 1, :] = n
        half = pl.ds(part * size, size)
        stores.append(fetch(res.at[half], out.at[half], out_sems.at[4 + part]))
    wait_all(stores)


def stats_kernel(
    heads, d, offsets, w, c0, c1, c2, c3, l_out, l_norm, gt, msg,
    w_buf, c_buf, l_buf, g_buf, sems, out_sems,
):
    tokens, width = c0.shape
    count = tokens // NEAR
    head = lax.axis_index("head")
    loads = []
    for flip, ref in enumerate((c0, c1, c2, c3)):
        first = pl.multiple_of(jnp.bitwise_xor(head, flip) * width, 128)
        loads.append(fetch(w.at[:, pl.ds(first, width)], w_buf.at[flip], sems.at[flip]))
        loads.append(fetch(ref, c_buf.at[flip], sems.at[4 + flip]))
    loads.append(fetch(l_out, l_buf, sems.at[8]))
    wait_all(loads[:4])
    grads = nt(w_buf[0], c_buf[0]) + nt(w_buf[1], c_buf[1])
    wait_all(loads[4:])
    grads = grads + nt(w_buf[2], c_buf[2]) + nt(w_buf[3], c_buf[3])
    grads = grads.astype(BF16)
    g_buf[...] = grads
    store = fetch(g_buf, gt, out_sems.at[0])
    for h in range(heads):
        rows = slice(h * d, (h + 1) * d)
        g = grads[rows].astype(F32)
        product = jnp.sum(g * l_buf[rows].astype(F32), axis=0, keepdims=True)
        stack = jnp.concatenate(
            [
                g,
                *split3(l_norm[h : h + 1, :]),
                *split3(product),
                jnp.zeros((122 - d, tokens), F32),
            ],
            axis=0,
        ).astype(BF16)
        near = nn(stack[:96], pick_matrix(tokens, count, offsets[0, h]))
        far = nt(place_matrix(tokens, 8, offsets[1, h], 16), stack)
        msg[h] = jnp.concatenate([near, far], axis=0).astype(BF16)
    store.wait()


def segment(got, first, size, part):
    pieces = [got[4 * part + z, first : first + size, :] for z in range(NEAR)]
    return jnp.concatenate(pieces, axis=1)


def overlap(near_offset, far_offset):
    shift = far_offset - near_offset
    spot = iota((8, 128), 0) * 16 + lax.shift_right_arithmetic(shift, 2)
    return (iota((8, 128), 1) == spot) & (lax.bitwise_and(shift, 3) == 0)


def near_forward_kernel(heads, d, factor, offsets, got, stats, msg, norm, shared, buf, sems):
    tokens = NEAR * got.shape[2]
    load = fetch(stats, buf, sems.at[0])
    diag = causal_mask(tokens // 2)
    same = overlap(*my_offsets(offsets, heads))
    hit = jnp.max(jnp.where(same, 1.0, 0.0), axis=1, keepdims=True) > 0.5
    twice = one_hot(jnp.concatenate([same, same], axis=0))
    lane = iota((8, 96), 1)
    stacks = []
    for part in range(2):
        qt, kt, vt = [segment(got, i * d, d, part) for i in range(3)]
        o, n = forward(qt, kt, vt, factor, diag)
        norm[part : part + 1, :] = n
        gap = jnp.zeros((6, tokens), F32)
        rest = jnp.zeros((87 - d, tokens), F32)
        stacks.append(jnp.concatenate([o, gap, *split3(n), rest], axis=0))
    load.wait()
    for part in range(2):
        for z in range(NEAR):
            spot = 4 * part + z
            piece = stacks[part][:, z * 128 : (z + 1) * 128]
            packed = piece.astype(BF16)
            msg[spot, :d] = buf[spot, :d]
            msg[spot, d : 2 * d] = packed[:d]
            both = buf[spot, d : d + 16].astype(F32) + piece[d:]
            msg[spot, 2 * d :] = both.astype(BF16)
            picked = nt(twice, packed)[:8]
            picked = jnp.where((lane == d + 6) & ~hit, LOW, picked)
            picked = jnp.concatenate([picked, jnp.zeros((8, 32), F32)], axis=1)
            rows = buf[spot, d + 16 :].astype(F32)[:8]
            rows = jnp.concatenate([picked, rows], axis=0).astype(BF16)
            for copy in range(shared.shape[0]):
                shared[copy, spot, :16] = got[spot, 3 * d :]
                shared[copy, spot, 16:] = rows


def far_block(got):
    rows = got[:, :, :16, :].astype(F32).reshape(64, 16, 128)
    wide = jnp.concatenate(
        [rows[:, :8].reshape(512, 128), rows[:, 8:].reshape(512, 128)], axis=1
    )
    return wide.T.astype(BF16)


def column_rows():
    return pl.ds(pl.multiple_of(lax.axis_index("seq") // 8 * 64, 64), 64)


def far_forward_kernel(d, factor, got, near, norm, msg, own, turned):
    block = far_block(got)
    tokens = block.shape[1]
    diag = causal_mask(tokens // 2)
    o, n = forward(block[:d], block[d : 2 * d], block[2 * d : 3 * d], factor, diag)
    norm[...] = jnp.broadcast_to(n, norm.shape)
    stack = jnp.concatenate([o, *split3(n), jnp.zeros((125 - d, tokens), F32)], axis=0)
    turned[...] = stack.T
    mine = turned[column_rows(), :].reshape(8, 8, 128)
    msg[:, : 2 * d + 16] = near[...]
    own[...] = mine
    rows = got[:, :, 16:, :].astype(F32)
    used = d + 6
    for h in range(msg.shape[0]):
        far = rows[:, h, 8:, :].reshape(64, 128)
        first = jnp.concatenate([far[:8, :used], mine[h, :, : 128 - used]], axis=1)
        tail = mine[h, :, 128 - used : 2 * (128 - used)]
        second = jnp.concatenate([far[8:16, :used], tail], axis=1)
        far = jnp.concatenate([first, second, far[16:]], axis=0)
        msg[h, 2 * d + 16 :] = far.astype(BF16)


def near_stats(d, stats, outs, part):
    g = segment(stats, 0, d, part).astype(F32)
    rest = segment(stats, 2 * d, 16, part).astype(F32)
    o = segment(outs, d, d, part).astype(F32)
    product = jnp.sum(g * o, axis=0, keepdims=True)
    return g, sum3(rest, 0, 0), sum3(rest, 3, 0), product


def owner_backward_kernel(
    heads, d, factor, scale, offsets, got, stats, mine, outs, near_norm, plane_got,
    far_norm, sent, rows_buf, turned, msg, sems,
):
    rows_buf[...] = stats[:, 2 * d + 16 : 2 * d + 80].astype(F32)
    near_offset, far_offset = my_offsets(offsets, heads)
    same = overlap(near_offset, far_offset)
    hit = jnp.max(jnp.where(same, 1.0, 0.0), axis=0, keepdims=True) > 0.5
    tokens = near_norm.shape[1]
    diag = causal_mask(tokens // 2)
    plane = pl.ds(pl.multiple_of(lax.axis_index("seq") // 8 * 8, 8), 8)
    lane = iota((8, 128), 1)
    for part in range(2):
        g, local_norm, local_dot, near_dot = near_stats(d, stats, outs, part)
        far_norms, far_dots = [], []
        for z in range(NEAR):
            rows = mine[4 * part + z]
            grads = rows_buf[4 * part + z, plane, :]
            dot = jnp.sum(jnp.where(lane < d, rows * grads, 0.0), axis=1, keepdims=True)
            log = jnp.sum(jnp.where(same, sum3(rows, d, 1), 0.0), axis=0, keepdims=True)
            far_norms.append(jnp.where(hit, log, NEG))
            far_dots.append(jnp.sum(jnp.where(same, dot, 0.0), axis=0, keepdims=True))
        extra = jnp.concatenate(far_norms, axis=1)
        extra_dot = jnp.concatenate(far_dots, axis=1)
        own = near_norm[part : part + 1, :]
        norm = log2_add(log2_add(own, local_norm), extra)
        delta = jnp.exp2(own - norm) * near_dot + jnp.exp2(local_norm - norm) * local_dot
        delta = delta + jnp.exp2(extra - norm) * extra_dot
        qt, kt, vt = [segment(got, i * d, d, part) for i in range(3)]
        grads = backward(qt, kt, vt, g.astype(BF16), norm, delta, factor, scale, diag)
        for slot in range(3):
            packed = grads[slot].astype(BF16)
            for z in range(NEAR):
                msg[4 * part + z, slot * d : (slot + 1) * d] = packed[:, z * 128 : (z + 1) * 128]
    near_part, far_part = pl.ds(0, 3 * d), pl.ds(3 * d, 16)
    store = fetch(msg.at[:, near_part], sent.at[:, near_part], sems.at[0])
    block = far_block(plane_got)
    qt, kt, vt = block[:d], block[d : 2 * d], block[2 * d : 3 * d]
    pieces = [rows_buf[z, 8 * a : 8 * a + 8, :] for a in range(8) for z in range(heads)]
    rows = jnp.concatenate(pieces, axis=0).T
    near = plane_got[:, :, 16:, :].astype(F32)[:, :, :8, :].reshape(tokens, 128).T
    gt = rows[:d].astype(BF16)
    local_norm, other_norm = sum3(rows, d, 0), sum3(near, d + 6, 0)
    own = far_norm[:1, :]
    norm = log2_add(log2_add(own, local_norm), other_norm)
    share = jnp.exp2(own - norm)
    rest = jnp.exp2(local_norm - norm) * sum3(rows, d + 3, 0)
    other = jnp.sum(rows[:d] * near[:d], axis=0, keepdims=True)
    rest = rest + jnp.exp2(other_norm - norm) * other
    dq, dk, dv = backward(qt, kt, vt, gt, own, rest, factor, scale, diag, share)
    stack = jnp.concatenate([dq, dk, dv, jnp.zeros((256 - 3 * d, tokens), F32)], axis=0)
    turned[...] = stack.T
    picked = turned[column_rows(), :]
    msg[:, 3 * d :] = jnp.concatenate(
        [picked[:, :128].reshape(8, 8, 128), picked[:, 128:].reshape(8, 8, 128)], axis=1
    ).astype(BF16)
    wait_all([store, fetch(msg.at[:, far_part], sent.at[:, far_part], sems.at[1])])


def local_backward_kernel(
    heads, d, factor, scale, offsets, qkvt, gt, l_out, l_norm, got, attended, grads,
    buf, o_buf, turned, rows_buf, res, sems, load_sems, out_sems,
):
    tokens = gt.shape[1]
    count = tokens // NEAR
    first = [fetch(l_out, o_buf, sems.at[0]), fetch(gt, buf.at[3], sems.at[1])]
    loads = [fetch(qkvt.at[i], buf.at[i], load_sems.at[i]) for i in range(3)]
    lane = iota((1, tokens), 1)
    diag = causal_mask(tokens // 2)
    wait_all(first)
    norms, deltas = [], []
    for h in range(heads):
        rows = slice(h * d, (h + 1) * d)
        near = nn(got[h, d : 2 * d + 16, :], place_matrix(tokens, count, offsets[0, h]))
        near_norm = jnp.where(lane % NEAR == offsets[0, h], sum3(near, d + 6, 0), NEG)
        place = iota((8, tokens), 1) == iota((8, tokens), 0) * 64 + offsets[1, h]
        came = got[h, 2 * d + 16 : 2 * d + 32, :].astype(F32)
        came = jnp.concatenate([came[:8, d + 6 :], came[8:, d + 6 :]], axis=1)
        spread = jnp.sum(jnp.where(place, sum3(came, d, 1), 0.0), axis=0, keepdims=True)
        far_norm = jnp.where(lane % 64 == offsets[1, h], spread, NEG)
        far_out = tn(came[:, :d].astype(BF16), one_hot(place))
        mine = l_norm[h : h + 1, :]
        both = log2_add(log2_add(mine, near_norm), far_norm)
        mixed = jnp.exp2(mine - both) * o_buf[rows].astype(F32)
        mixed = mixed + jnp.exp2(near_norm - both) * near[:d]
        mixed = (mixed + jnp.exp2(far_norm - both) * far_out).astype(BF16)
        turned[rows, :] = mixed
        delta = buf[3, rows].astype(F32) * mixed.astype(F32)
        norms.append(both)
        deltas.append(jnp.sum(delta, axis=0, keepdims=True))
    rows_buf[...] = turned[...].T
    store = fetch(rows_buf, attended, out_sems.at[0])
    wait_all(loads)
    size = heads // 2 * d
    stores = [store]
    for part in range(2):
        for h in range(part * heads // 2, (part + 1) * heads // 2):
            rows = slice(h * d, (h + 1) * d)
            parts = backward(
                buf[0, rows], buf[1, rows], buf[2, rows], buf[3, rows],
                norms[h], deltas[h], factor, scale, diag,
            )
            for slot in range(3):
                res[slot, rows] = parts[slot].astype(res.dtype)
        half = pl.ds(part * size, size)
        for slot in range(3):
            stores.append(
                fetch(res.at[slot, half], grads.at[slot, half], out_sems.at[1 + 3 * part + slot])
            )
    wait_all(stores)


def final_kernel(heads, d, offsets, grads, got, dq, dk, dv, turned, rows_buf, out_sems):
    tokens = grads.shape[2]
    count = tokens // NEAR
    for h in range(heads):
        rows = slice(h * d, (h + 1) * d)
        total = nn(got[h, : 3 * d], place_matrix(tokens, count, offsets[0, h]))
        place = one_hot(iota((8, tokens), 1) == iota((8, tokens), 0) * 64 + offsets[1, h])
        far = got[h, 3 * d :].astype(F32)
        far = jnp.concatenate([far[:8], far[8:]], axis=1).astype(BF16)
        total = total + tn(far, place)[: 3 * d]
        for slot in range(3):
            mine = total[slot * d : (slot + 1) * d] + grads[slot, rows].astype(F32)
            turned[slot, rows, :] = mine.astype(BF16)
    stores = []
    for slot, ref in enumerate((dq, dk, dv)):
        rows_buf[slot] = turned[slot].T
        stores.append(fetch(rows_buf.at[slot], ref, out_sems.at[slot]))
    wait_all(stores)


def call(kernel, name, operands, outs, scratch=(), limit=63_000_000):
    spaces = {"s": pltpu.SMEM, "v": pltpu.VMEM, "h": pltpu.HBM}
    arrays = [x for x, _ in operands]
    shapes = [x for x, _ in outs]
    return pl.pallas_call(
        kernel,
        name=name,
        out_shape=shapes,
        in_specs=[pl.BlockSpec(memory_space=spaces[where]) for _, where in operands],
        out_specs=[pl.BlockSpec(memory_space=spaces[where]) for _, where in outs],
        scratch_shapes=list(scratch),
        compiler_params=pltpu.CompilerParams(vmem_limit_bytes=limit),
        cost_estimate=pl.CostEstimate(flops=1000, bytes_accessed=1000, transcendentals=0),
    )(*arrays)


def after(x, y):
    return lax.optimization_barrier((x, y))[0]


def on_device(query_rows, key_rows, value_rows, out_weight, cotangent, offsets):
    tokens, width = query_rows.shape
    heads = offsets.shape[1]
    d = width // heads
    scale = 1.0 / math.sqrt(d)
    factor = scale * LOG2E
    seq_size = lax.axis_size("seq")
    count = tokens // NEAR
    groups = seq_size // heads
    columns = [[a * heads + z for z in range(heads)] for a in range(groups)]
    planes = [[a * heads + z for a in range(groups)] for z in range(heads)]
    struct = jax.ShapeDtypeStruct
    dma = pltpu.SemaphoreType.DMA

    def vmem(*shape, dtype=BF16):
        return pltpu.VMEM(shape, dtype)

    def along_column(x):
        return lax.all_to_all(x, "seq", 0, 0, tiled=True, axis_index_groups=columns)

    def over_plane(copies):
        return lax.all_to_all(copies, "seq", 0, 0, tiled=True, axis_index_groups=planes)

    def flipped(x, bit):
        return lax.ppermute(x, "head", [(i, i ^ bit) for i in range(4)])

    c2 = flipped(cotangent, 2)
    c1 = flipped(cotangent, 1)
    qkvt, rows_msg, l_out, l_norm = call(
        functools.partial(local_kernel, heads, factor),
        "local_forward",
        [(offsets, "s"), (query_rows, "h"), (key_rows, "h"), (value_rows, "h")],
        [
            (struct((3, width, tokens), BF16), "h"),
            (struct((heads, 256, count), BF16), "h"),
            (struct((width, tokens), BF16), "h"),
            (struct((heads, tokens), F32), "v"),
        ],
        scratch=[
            vmem(3, tokens, width),
            vmem(3, width, tokens),
            vmem(heads, 256, count),
            vmem(width, tokens),
            dma((3,)),
            dma((6,)),
        ],
    )
    rows_got = along_column(rows_msg)
    c2 = after(c2, l_norm)
    c3 = flipped(c2, 1)
    gt, stats_msg = call(
        functools.partial(stats_kernel, heads, d),
        "stats",
        [(offsets, "s"), (out_weight, "h")]
        + [(x, "h") for x in (cotangent, c1, c2, c3)]
        + [(l_out, "h"), (l_norm, "v")],
        [
            (struct((width, tokens), BF16), "h"),
            (struct((heads, 112, 128), BF16), "v"),
        ],
        scratch=[
            vmem(4, width, width),
            vmem(4, tokens, width),
            vmem(width, tokens),
            vmem(width, tokens),
            dma((9,)),
            dma((1,)),
        ],
    )
    rows_got = after(rows_got, stats_msg)
    near_out, near_norm, shared = call(
        functools.partial(near_forward_kernel, heads, d, factor),
        "near_forward",
        [(offsets, "s"), (rows_got, "v"), (stats_msg, "h")],
        [
            (struct((heads, 176, count), BF16), "v"),
            (struct((2, tokens), F32), "v"),
            (struct((groups, heads, 32, 128), BF16), "v"),
        ],
        scratch=[vmem(heads, 112, 128), dma((1,))],
        limit=16_000_000,
    )
    far_got = over_plane(shared)
    far_norm, swap_msg, own_far = call(
        functools.partial(far_forward_kernel, d, factor),
        "far_forward",
        [(far_got, "v"), (near_out, "v")],
        [
            (struct((8, tokens), F32), "v"),
            (struct((heads, 240, 128), BF16), "v"),
            (struct((heads, 8, 128), F32), "v"),
        ],
        scratch=[vmem(tokens, 128, dtype=F32)],
        limit=16_000_000,
    )
    swap_got = along_column(swap_msg)
    (grad_msg,) = call(
        functools.partial(owner_backward_kernel, heads, d, factor, scale),
        "owner_backward",
        [(offsets, "s"), (rows_got, "v"), (swap_got, "v"), (own_far, "v"), (near_out, "v")]
        + [(near_norm, "v"), (far_got, "v"), (far_norm, "v")],
        [(struct((heads, 256, 128), BF16), "h")],
        scratch=[
            vmem(heads, 64, 128, dtype=F32),
            vmem(tokens, 256, dtype=F32),
            vmem(heads, 256, 128),
            dma((2,)),
        ],
        limit=16_000_000,
    )
    owner_grads = along_column(grad_msg)
    swap_got = after(swap_got, grad_msg)
    attended, grads = call(
        functools.partial(local_backward_kernel, heads, d, factor, scale),
        "local_backward",
        [(offsets, "s"), (qkvt, "h"), (gt, "h"), (l_out, "h"), (l_norm, "v"), (swap_got, "v")],
        [
            (struct((tokens, width), BF16), "h"),
            (struct((3, width, tokens), BF16), "h"),
        ],
        scratch=[
            vmem(4, width, tokens),
            vmem(width, tokens),
            vmem(width, tokens),
            vmem(tokens, width),
            vmem(3, width, tokens),
            dma((2,)),
            dma((3,)),
            dma((7,)),
        ],
    )
    grad_query, grad_key, grad_value = call(
        functools.partial(final_kernel, heads, d),
        "final",
        [(offsets, "s"), (grads, "v"), (owner_grads, "v")],
        [(struct((tokens, width), BF16), "h")] * 3,
        scratch=[
            vmem(3, width, tokens),
            vmem(3, tokens, width),
            dma((3,)),
        ],
        limit=16_000_000,
    )
    return (attended, grad_query, grad_key, grad_value)


def solution(mesh):
    return jax.shard_map(
        on_device,
        mesh=mesh,
        in_specs=(
            P("seq", "head"),
            P("seq", "head"),
            P("seq", "head"),
            P("head", None),
            P("seq", "head"),
            P(None, "head"),
        ),
        out_specs=(P("seq", "head"), P("seq", "head"), P("seq", "head"), P("seq", "head")),
        check_vma=False,
    )
```
